128 devices in a mesh: dp: 16 (over z, x_hi, core), tensor: 8 (over x_lo, y).
Axes of the slice: x: 4 (x_hi: 2, x_lo: 2; x = x_hi * 2 + x_lo), y: 4, z: 4, core: 2. Of those that a mesh axis runs over, the one named last changes fastest.
Arguments:
- tokens: bfloat16 [16384, 1024], P(('dp', 'tensor')), may hold values from -6 to 6
- attn_in: bfloat16 [1024, 3, 16, 64], P(None, None, 'tensor'), may hold values from -0.25 to 0.25
- attn_out: bfloat16 [16, 64, 1024], P('tensor'), may hold values from -1 to 1
- mlp_in: bfloat16 [2, 1024, 2624], P(None, None, 'tensor'), may hold values from -0.1875 to 0.1875
- mlp_out: bfloat16 [2624, 1024], P('tensor'), may hold values from -0.25 to 0.25
- norm_first: float32 [1024], replicated, may hold values from 0.5 to 1.5
- norm_second: float32 [1024], replicated, may hold values from 0.5 to 1.5
- cotangent: bfloat16 [16384, 1024], P(('dp', 'tensor')), may hold values from -6 to 6
Outputs:
- layer_output: bfloat16 [16384, 1024], P(('dp', 'tensor'))
- tokens_grad: float32 [16384, 1024], P(('dp', 'tensor'))
- attn_in_grad: float32 [1024, 3, 16, 64], P(None, None, 'tensor')
- attn_out_grad: float32 [16, 64, 1024], P('tensor')
- mlp_in_grad: float32 [2, 1024, 2624], P(None, None, 'tensor')
- mlp_out_grad: float32 [2624, 1024], P('tensor')
- norm_first_grad: float32 [1024], replicated
- norm_second_grad: float32 [1024], replicated
The draws below stay inside these ranges and needn't reach their ends.
All inputs are finite; a program needn't handle non-finite values.
Results may differ from the reference program's by a relative error of at most 0.03.
Values may be sent and summed in bfloat16 or wider, within the bound.
A program may use at most 128 MiB of HBM per device.

```python
import math
import jax
import jax.numpy as jnp
from jax import lax

D = 1024
H = 16
HD = 64
FF = 2624
SEQ_LEN = 1024
SEQUENCES = 16
TOKENS = 16384


def level_of(rng, extent, shards, smallest, high):
    factor_of = 1.0
    for position, shards_of in shards:
        draws = jax.random.uniform(jax.random.fold_in(jax.random.fold_in(rng, 6), position), (shards_of,), jnp.float32, smallest / len(shards), high / len(shards))
        factor_of = factor_of * jnp.repeat(jnp.exp(draws), extent[position] // shards_of).reshape((-1,) + (1,) * (len(extent) - 1 - position))
    return factor_of


def bell_draw(own_key, shape, width, bound, split=(), kind=jnp.bfloat16):
    values = jax.random.normal(own_key, shape, jnp.float32) * width
    if len(split) > 0:
        values = level_of(own_key, shape, split, -0.22, 0.18) * values
    return jnp.clip(values, min=-bound, max=bound).astype(kind)


def setup_inputs(seed: int = 0) -> dict:
    splits = jax.random.split(jax.random.key(seed), 9)
    tokens = bell_draw(splits[0], (TOKENS, D), 1.0, 6.0, ((0, 128),))
    attn_in = bell_draw(splits[1], (D, 3, H, HD), (D // 2) ** -0.5, 0.25, ((2, 8),))
    attn_out = bell_draw(splits[2], (H, HD, D), 32 ** -0.5, 1.0, ((0, 8),))
    mlp_in = bell_draw(splits[3], (2, D, FF), D ** -0.5, 0.1875, ((2, 8),))
    mlp_out = bell_draw(splits[4], (FF, D), (FF // 4) ** -0.5, 0.25, ((0, 8),))
    norm_first = jnp.clip(1.0 + 0.1 * jax.random.normal(splits[5], (D,), jnp.float32), 0.5, 1.5)
    norm_second = jnp.clip(1.0 + 0.1 * jax.random.normal(splits[6], (D,), jnp.float32), 0.5, 1.5)
    cotangent = bell_draw(splits[7], (TOKENS, D), 1.0, 6.0, ((0, 128),))
    return {"tokens": tokens, "attn_in": attn_in, "attn_out": attn_out, "mlp_in": mlp_in, "mlp_out": mlp_out, "norm_first": norm_first, "norm_second": norm_second, "cotangent": cotangent}


EPS = 1e-05
THETA = 160000.0
HIGHEST = lax.Precision.HIGHEST

@jax.custom_vjp
def low(v):
    return lax.optimization_barrier(v.astype(jnp.bfloat16)).astype(jnp.float32)

@jax.custom_vjp
def low_back(v):
    return v

def low_keep(v):
    return (low(v), None)

def low_pass(kept, grad):
    return (grad,)

def back_keep(v):
    return (v, None)

def back_low(kept, grad):
    return (low(grad),)
low.defvjp(low_keep, low_pass)
low_back.defvjp(back_keep, back_low)

def rope_tables(length, head_size):
    places = jnp.arange(length, dtype=jnp.float32)
    frequency = THETA ** (-jnp.arange(0, head_size, 2, dtype=jnp.float32) / head_size)
    angles = places[:, None] * frequency[None, :]
    cosine = jnp.concatenate([jnp.cos(angles), jnp.cos(angles)], -1)
    sine_table = jnp.concatenate([jnp.sin(angles), jnp.sin(angles)], -1)
    return (cosine[:, None, :], sine_table[:, None, :])

def rotate(values, cosine, sine_table):
    half_size = values.shape[-1] // 2
    turned = jnp.concatenate([-values[..., half_size:], values[..., :half_size]], -1)
    return values * cosine + turned * sine_table

def layer_norm(values, gain_vector):
    row_mean = lax.optimization_barrier(jnp.mean(values, -1, keepdims=True))
    centred = values - row_mean
    variance = lax.optimization_barrier(jnp.mean(centred * centred, -1, keepdims=True))
    return centred * lax.rsqrt(variance + EPS) * gain_vector

def attention(queries, key_rows, value_rows):
    group, length, head_count, head_size = queries.shape
    block_rows = min(512, length)
    block_count = length // block_rows
    score_scale = head_size ** (-0.5)
    blocked = queries.reshape(group, block_count, block_rows, head_count, head_size).transpose(1, 0, 2, 3, 4)

    def one_block(query_block):
        scores = jnp.einsum('gqhe,gkhe->ghqk', query_block, key_rows, precision=HIGHEST) * score_scale
        scores = low_back(scores)
        top_score = lax.optimization_barrier(jnp.max(scores, -1, keepdims=True))
        powers = jnp.exp(scores - top_score)
        probs = low(powers / lax.optimization_barrier(jnp.sum(powers, -1, keepdims=True)))
        return jnp.einsum('ghqk,gkhe->gqhe', probs, value_rows, precision=HIGHEST)
    result = lax.map(jax.checkpoint(one_block), blocked)
    return result.transpose(1, 0, 2, 3, 4).reshape(group, length, head_count, head_size)

def forward(inflow, attn_in, attn_out, mlp_in, mlp_out, norm_first, norm_second):
    length = inflow.shape[1]
    cosine, sine_table = rope_tables(length, attn_in.shape[3])
    first_hidden = low(layer_norm(inflow, norm_first))
    projected = low_back(jnp.einsum('gld,dthe->glthe', first_hidden, attn_in, precision=HIGHEST))
    queries = low(rotate(projected[:, :, 0], cosine, sine_table))
    key_rows = low(rotate(projected[:, :, 1], cosine, sine_table))
    value_rows = low(projected[:, :, 2])
    attended = low_back(low(attention(queries, key_rows, value_rows)))
    branch_attn = low_back(jnp.einsum('glhe,hed->gld', attended, attn_out, precision=HIGHEST))
    middle = inflow + branch_attn
    second_hidden = low(layer_norm(middle, norm_second))
    gate_up = low_back(jnp.einsum('gld,tdf->tglf', second_hidden, mlp_in, precision=HIGHEST))
    mixed = low_back(low(jax.nn.gelu(gate_up[0], approximate=False) * gate_up[1]))
    branch_mlp = low_back(jnp.einsum('glf,fd->gld', mixed, mlp_out, precision=HIGHEST))
    return middle + branch_mlp

def reference(tokens, attn_in, attn_out, mlp_in, mlp_out, norm_first, norm_second, cotangent):
    group = math.gcd(SEQUENCES, max(1, 4096 // SEQ_LEN))
    step_count = SEQUENCES // group
    inputs = tokens.astype(jnp.float32).reshape(step_count, group, SEQ_LEN, D)
    upstreams = cotangent.astype(jnp.float32).reshape(step_count, group, SEQ_LEN, D)
    weight_set = (attn_in.astype(jnp.float32), attn_out.astype(jnp.float32), mlp_in.astype(jnp.float32), mlp_out.astype(jnp.float32), norm_first.astype(jnp.float32), norm_second.astype(jnp.float32))

    def one_group(totals, pieces):
        inflow, upstream = pieces
        result, pullback = jax.vjp(forward, inflow, *weight_set)
        gradients = pullback(upstream)
        totals = tuple((partial_sum + addend for partial_sum, addend in zip(totals, gradients[1:])))
        return (totals, (result.astype(jnp.bfloat16), gradients[0]))
    zero_sums = tuple((jnp.zeros_like(member) for member in weight_set))
    totals, (outputs, input_grads) = lax.scan(one_group, zero_sums, (inputs, upstreams))
    return (outputs.reshape(TOKENS, D), input_grads.reshape(TOKENS, D), totals[0], totals[1], totals[2], totals[3], totals[4], totals[5])
```

```python
import jax
import jax.numpy as jnp
import numpy as np
from jax import lax
from jax.experimental import pallas as pl
from jax.experimental.pallas import tpu as pltpu
from jax.sharding import PartitionSpec as P

MESH = pl.DeviceIdType.MESH
BF = jnp.bfloat16
F32 = jnp.float32
EPS = 1e-05
THETA = 160000.0
T = 1024
D = 1024
B = 128
FF = 328
FP = 384
FR = 336


def tables():
    places = np.arange(T, dtype=np.float32)
    frequency = (THETA ** (-np.arange(0, 64, 2, dtype=np.float32) / 64)).astype(np.float32)
    angles = places[:, None] * frequency[None, :]
    cosine, sine = np.cos(angles), np.sin(angles)
    cosine = np.concatenate([cosine, cosine] * 2, -1)
    signed = np.concatenate([-sine, sine] * 2, -1)
    order = np.concatenate([np.arange(B) + ((j % 2) * 4 + j // 2) * B for j in range(8)])
    return cosine[order].astype(np.float32), signed[order].astype(np.float32)


def nn(a, b):
    return jnp.dot(a, b, preferred_element_type=F32)


def nt(a, b):
    return lax.dot_general(a, b, (((1,), (1,)), ((), ())), preferred_element_type=F32)


def swap_halves(u):
    lane = lax.broadcasted_iota(jnp.int32, u.shape, 1)
    return jnp.where((lane % 64) < 32, pltpu.roll(u, 96, 1), pltpu.roll(u, 32, 1))


def norm(v):
    centred = v - jnp.mean(v, -1, keepdims=True)
    inverse = lax.rsqrt(jnp.mean(centred * centred, -1, keepdims=True) + EPS)
    return centred * inverse, inverse


def norm_back(gradient, xhat, inverse, gain):
    e = gradient * gain
    dx = inverse * (
        e - jnp.mean(e, -1, keepdims=True) - xhat * jnp.mean(e * xhat, -1, keepdims=True)
    )
    return dx, jnp.sum(gradient * xhat, 0, keepdims=True)


def rows(start, size):
    return pl.ds(pl.multiple_of(start, 16), size)


def cols(start, size):
    return pl.ds(pl.multiple_of(start, 128), size)


def remote(src, dst, ssem, rsem, dev):
    return pltpu.make_async_remote_copy(
        src_ref=src, dst_ref=dst, send_sem=ssem, recv_sem=rsem, device_id=dev, device_id_type=MESH
    )


class Place:
    def __init__(self):
        dp, tensor = lax.axis_index("dp"), lax.axis_index("tensor")
        self.dp, self.tensor = dp, tensor
        self.c = dp % 2
        self.xlo, self.y = tensor // 4, tensor % 4
        self.z = dp // 4
        self.x = ((dp // 2) % 2) * 2 + self.xlo
        self.me = 2 * self.y + self.c
        self.mover = self.c != self.xlo
        self.right, self.left = (self.y + 1) % 4, (self.y + 3) % 4
        self.opp = (self.y + 2) % 4

    def team(self, core, y):
        return {"dp": self.dp - self.c + core, "tensor": self.xlo * 4 + y}

    def plane(self, x, z, core=None):
        core = self.c if core is None else core
        return {"dp": z * 4 + (x // 2) * 2 + core, "tensor": (x % 2) * 4 + self.y}

    def partner(self):
        return {"dp": self.dp - self.c + self.xlo, "tensor": self.c * 4 + self.y}


class Gather:
    def __init__(self, place, buf, ssem, rsem):
        self.p, self.buf, self.ssem, self.rsem = place, buf, ssem, rsem

    def msg(self, i):
        p = self.p
        me, lt, rt, op = p.me, 2 * p.left + p.c, 2 * p.right + p.c, 2 * p.opp + p.c
        right, left = p.team(p.c, p.right), p.team(p.c, p.left)
        sib = p.team(1 - p.c, p.y)
        block, first, size, dev = (
            (me, 0, 64, right),
            (me, 64, 64, left),
            (me, 64, 64, right),
            (me, 0, 64, left),
            (me, 0, 128, sib),
            (lt, 0, 64, right),
            (rt, 64, 64, left),
            (lt, 0, 128, sib),
            (rt, 0, 128, sib),
            (op, 0, 64, sib),
            (op, 64, 64, sib),
        )[i]
        ref = self.buf.at[rows(block * B + first, size)]
        return remote(ref, ref, self.ssem.at[i], self.rsem.at[i], dev)

    def start(self):
        for i in range(5):
            self.msg(i).start()

    def first(self):
        self.msg(4).wait_recv()

    def second(self):
        self.msg(0).wait_recv()
        self.msg(5).start()
        self.msg(1).wait_recv()
        self.msg(6).start()
        self.msg(2).wait_recv()
        self.msg(7).start()
        self.msg(3).wait_recv()
        self.msg(8).start()

    def third(self):
        self.msg(5).wait_recv()
        self.msg(9).start()
        self.msg(6).wait_recv()
        self.msg(10).start()

    def left_in(self):
        self.msg(7).wait_recv()

    def right_in(self):
        self.msg(8).wait_recv()

    def opp_in(self):
        self.msg(9).wait_recv()
        self.msg(10).wait_recv()

    def sent(self):
        for i in range(11):
            self.msg(i).wait_send()

    def rest(self):
        self.left_in()
        self.right_in()
        self.opp_in()
        self.sent()

    def steps(self, body):
        p = self.p

        @pl.loop(0, 4)
        def _(step):
            @pl.when(step == 0)
            def _():
                self.first()

            @pl.when(step == 1)
            def _():
                self.second()
                self.left_in()

            @pl.when(step == 2)
            def _():
                self.right_in()

            @pl.when(step == 3)
            def _():
                self.third()
                self.opp_in()

            off = jnp.where(step == 0, 0, jnp.where(step == 1, 3, jnp.where(step == 2, 1, 2)))
            body((p.y + off) % 4)

        self.sent()


class Scatter:
    def __init__(self, place, part, got, held, top, bottom, from_left, from_right, ssem, rsem):
        self.p = place
        self.part, self.got, self.held = part, got, held
        self.top, self.bottom = top, bottom
        self.from_left, self.from_right = from_left, from_right
        self.ssem, self.rsem = ssem, rsem

    def off(self, step):
        return jnp.where(step == 0, 2, jnp.where(step == 1, 1, jnp.where(step == 2, 3, 0)))

    def sib(self, step):
        p = self.p
        yy = (p.y + self.off(step)) % 4
        return remote(
            self.part.at[rows((2 * yy + 1 - p.c) * B, B)],
            self.got.at[rows(yy * B, B)],
            self.ssem.at[step],
            self.rsem.at[step],
            p.team(1 - p.c, p.y),
        )

    def msg(self, i):
        p = self.p
        right, left = p.team(p.c, p.right), p.team(p.c, p.left)
        block, first, dst, dev = (
            (p.opp, 0, self.top, right),
            (p.opp, 64, self.bottom, left),
            (p.right, 64, self.from_left.at[rows(64, 64)], right),
            (p.right, 0, self.from_left.at[rows(0, 64)], right),
            (p.left, 0, self.from_right.at[rows(0, 64)], left),
            (p.left, 64, self.from_right.at[rows(64, 64)], left),
        )[i]
        return remote(
            self.held.at[rows(block * B + first, 64)], dst, self.ssem.at[4 + i], self.rsem.at[4 + i], dev
        )

    def phase(self, compute):
        p = self.p

        @pl.loop(0, 4)
        def _(step):
            yy = (p.y + self.off(step)) % 4
            self.part[rows(yy * 256, 256), :] = compute(yy).astype(BF)
            self.sib(step).start()

    def pair_sum(self, yy):
        own = self.part[rows((2 * yy + self.p.c) * B, B), :].astype(F32)
        return own + self.got[rows(yy * B, B), :].astype(F32)

    def step0(self):
        p = self.p
        self.sib(0).wait_recv()
        self.held[rows(p.opp * B, B), :] = self.pair_sum(p.opp).astype(BF)
        self.msg(0).start()
        self.msg(1).start()

    def step1(self):
        p = self.p
        self.sib(1).wait_recv()
        total = self.pair_sum(p.right)
        self.held[rows(p.right * B + 64, 64), :] = total[64:].astype(BF)
        self.msg(2).start()
        self.sib(2).wait_recv()
        total2 = self.pair_sum(p.left)
        self.held[rows(p.left * B, 64), :] = total2[:64].astype(BF)
        self.msg(4).start()
        self.msg(0).wait_recv()
        self.held[rows(p.right * B, 64), :] = (total[:64] + self.top[...].astype(F32)).astype(BF)
        self.msg(3).start()
        self.msg(1).wait_recv()
        self.held[rows(p.left * B + 64, 64), :] = (total2[64:] + self.bottom[...].astype(F32)).astype(BF)
        self.msg(5).start()

    def step2(self):
        p = self.p
        self.sib(3).wait_recv()
        total = self.pair_sum(p.y)
        for i in range(2, 6):
            self.msg(i).wait_recv()
        total = total + self.from_left[...].astype(F32) + self.from_right[...].astype(F32)
        for i in range(4):
            self.sib(i).wait_send()
        for i in range(6):
            self.msg(i).wait_send()
        return total


class Sums:
    def __init__(self, place, full, slots, mine, out, size, ssem, rsem, bsem, esem):
        self.p = place
        self.full, self.slots, self.mine, self.out = full, slots, mine, out
        self.size = size
        self.ssem, self.rsem, self.bsem, self.esem = ssem, rsem, bsem, esem

    def peer(self, k):
        return (self.p.x + k % 4) % 4, (self.p.z + k // 4) % 4

    def spread_msg(self, k):
        x, z = self.peer(k)
        return remote(
            self.full.at[rows((z * 4 + x) * self.size, self.size)],
            self.slots.at[rows(k * self.size, self.size)],
            self.ssem.at[k],
            self.rsem.at[k],
            self.p.plane(x, z),
        )

    def spread(self):
        @pl.loop(1, 16)
        def _(k):
            self.spread_msg(k).start()

    def add(self):
        p, size = self.p, self.size

        @pl.loop(1, 16)
        def _(k):
            self.spread_msg(k).wait_recv()

        @pl.loop(0, size // 16)
        def _(r):
            total = self.full[rows((p.z * 4 + p.x) * size + r * 16, 16), :].astype(F32)
            for k in range(1, 16):
                total = total + self.slots[rows(k * size + r * 16, 16), :].astype(F32)
            self.mine[rows(r * 16, 16), :] = total.astype(BF)

        @pl.loop(1, 16)
        def _(k):
            self.spread_msg(k).wait_send()

    def return_msg(self, k):
        p = self.p
        x, z = self.peer(k)
        return remote(
            self.mine,
            self.out.at[rows((p.z * 4 + p.x) * self.size, self.size)],
            self.bsem.at[k],
            self.bsem.at[16 + k],
            p.plane(x, z),
        )

    def goes(self, k):
        return ((self.p.x + k % 4) % 2 == self.p.c) & (k != 0)

    def give(self):
        p = self.p

        @pl.loop(0, 16)
        def _(k):
            @pl.when(self.goes(k))
            def _():
                self.return_msg(k).start()

        @pl.when(jnp.logical_not(p.mover))
        def _():
            self.out[rows((p.z * 4 + p.x) * self.size, self.size), :] = self.mine[...]

    def forward(self):
        p = self.p
        return remote(self.out, self.out, self.esem.at[0], self.esem.at[1], p.team(1 - p.c, p.y))

    def take(self):
        p = self.p

        @pl.when(jnp.logical_not(p.mover))
        def _():
            @pl.loop(1, 16)
            def _(k):
                self.return_msg(k).wait_recv()

            self.forward().start()

    def finish(self):
        p = self.p

        @pl.when(p.mover)
        def _():
            self.forward().wait_recv()

        @pl.when(jnp.logical_not(p.mover))
        def _():
            self.forward().wait_send()

        @pl.loop(0, 16)
        def _(k):
            @pl.when(self.goes(k))
            def _():
                self.return_msg(k).wait_send()


class Gain:
    def __init__(self, place, team_buf, plane_buf, sems):
        self.p, self.team_buf, self.plane_buf, self.sems = place, team_buf, plane_buf, sems

    def team_msg(self, k):
        p = self.p
        j = (p.me + k) % 8
        ref = self.team_buf.at[p.me]
        return remote(ref, ref, self.sems.at[0, k], self.sems.at[1, k], p.team(j % 2, j // 2))

    def plane_msg(self, k):
        p = self.p
        x, z = (p.x + k % 4) % 4, (p.z + k // 4) % 4
        ref = self.plane_buf.at[p.z * 4 + p.x]
        return remote(ref, ref, self.sems.at[2, k], self.sems.at[3, k], p.plane(x, z))

    def start(self, value):
        self.team_buf[self.p.me] = value

        @pl.loop(1, 8)
        def _(k):
            self.team_msg(k).start()

    def middle(self):
        @pl.loop(1, 8)
        def _(k):
            self.team_msg(k).wait_recv()

        self.plane_buf[self.p.z * 4 + self.p.x] = jnp.sum(self.team_buf[...], 0)

        @pl.loop(1, 16)
        def _(k):
            self.plane_msg(k).start()

        @pl.loop(1, 8)
        def _(k):
            self.team_msg(k).wait_send()

    def end(self):
        @pl.loop(1, 16)
        def _(k):
            self.plane_msg(k).wait_recv()

        total = jnp.sum(self.plane_buf[...], 0)

        @pl.loop(1, 16)
        def _(k):
            self.plane_msg(k).wait_send()

        return total


class Swap:
    def __init__(self, place, src, dst, sems, there=None):
        self.p, self.src, self.dst, self.sems = place, src, dst, sems
        self.there = dst if there is None else there

    def far(self):
        return remote(self.src, self.there, self.sems.at[0], self.sems.at[1], self.p.partner())

    def near(self):
        return pltpu.make_async_copy(self.src, self.dst, self.sems.at[2])

    def start(self):
        pl.when(self.p.mover)(lambda: self.far().start())
        pl.when(jnp.logical_not(self.p.mover))(lambda: self.near().start())

    def wait(self):
        pl.when(self.p.mover)(lambda: self.far().wait())
        pl.when(jnp.logical_not(self.p.mover))(lambda: self.near().wait())


class Fetch:
    def __init__(self, place, src, dst, halves, sems, there=None):
        self.p, self.src, self.dst, self.halves, self.sems = place, src, dst, halves, sems
        self.there = dst if there is None else there

    def far(self, i):
        p = self.p
        x = (p.x + (1, 3)[i]) % 4
        part = self.halves[i]
        return remote(
            self.src.at[part],
            self.there.at[part],
            self.sems.at[i],
            self.sems.at[2 + i],
            p.plane(x, p.z, p.xlo),
        )

    def near(self):
        return pltpu.make_async_copy(self.src, self.dst, self.sems.at[4])

    def start(self):
        @pl.when(self.p.mover)
        def _():
            self.far(0).start()
            self.far(1).start()

        pl.when(jnp.logical_not(self.p.mover))(lambda: self.near().start())

    def wait(self):
        @pl.when(self.p.mover)
        def _():
            self.far(0).wait()
            self.far(1).wait()

        pl.when(jnp.logical_not(self.p.mover))(lambda: self.near().wait())


class Exchange:
    def __init__(self, place, src_of, dst, ssem, rsem):
        self.p, self.src_of, self.dst = place, src_of, dst
        self.ssem, self.rsem = ssem, rsem

    def msg(self, k):
        p = self.p
        j = (p.me + k) % 8
        return remote(
            self.src_of(j), self.dst, self.ssem.at[k], self.rsem.at[k], p.team(j % 2, j // 2)
        )

    def start(self):
        @pl.loop(1, 8)
        def _(k):
            self.msg(k).start()

    def wait(self):
        @pl.loop(1, 8)
        def _(k):
            self.msg(k).wait_recv()

        @pl.loop(1, 8)
        def _(k):
            self.msg(k).wait_send()


SCRATCH = dict(
    xb=((B, D), BF),
    cotb=((T, D), BF),
    w=((D, 384), BF),
    wo=((T, D), BF),
    wg=((2, D, FP), BF),
    wm=((FP, D), BF),
    h1=((T, D), BF),
    h2=((T, D), BF),
    gb=((T, D), BF),
    xhat1=((B, D), F32),
    inv1=((B, 1), F32),
    y1=((B, D), F32),
    xhat2=((B, D), F32),
    inv2=((B, 1), F32),
    gy=((B, D), F32),
    q=((T, B), BF),
    qt=((2, B, T), BF),
    k=((T, B), BF),
    kt=((B, T), BF),
    v=((T, B), BF),
    vt=((B, T), BF),
    pt=((2, T, T), BF),
    ot=((B, T), F32),
    o=((T, B), BF),
    orow=((B, D), BF),
    dorow=((B, D), BF),
    dob=((T, B), BF),
    dot=((2, B, T), BF),
    dsum=((2, 1, T), F32),
    ds=((T, T), BF),
    dqt=((B, T), F32),
    dk=((T, B), F32),
    dv=((T, B), F32),
    dqkv=((T, 384), BF),
    dqkvt=((384, T), BF),
    m=((T, FP), BF),
    da=((T, FP), BF),
    db=((T, FP), BF),
    mt=((FP, T), BF),
    dat=((FP, T), BF),
    dbt=((FP, T), BF),
    gm=((1024, D), BF),
    gm_slots=((1024, D), BF),
    gm_mine=((64, D), BF),
    gm_out=((1024, D), BF),
    ga=((512, D), BF),
    ga_slots=((512, D), BF),
    ga_mine=((32, D), BF),
    ga_out=((512, D), BF),
    g1t=((8, 1, D), F32),
    g1p=((16, 1, D), F32),
    g2t=((8, 1, D), F32),
    g2p=((16, 1, D), F32),
    lo_here=((B, D), BF),
    lo_out=((B, D), BF),
    tg_here=((B, D), BF),
    tg_out=((B, D), BF),
)
for _name in ("r2", "ro", "r1"):
    SCRATCH.update(
        {
            _name + "_part": ((T, D), BF),
            _name + "_got": ((512, D), BF),
            _name + "_held": ((512, D), BF),
            _name + "_top": ((64, D), BF),
            _name + "_bottom": ((64, D), BF),
            _name + "_left": ((B, D), BF),
            _name + "_right": ((B, D), BF),
        }
    )
SEMS = dict(
    ag_h1=(2, 11), ag_wo=(2, 11), ag_cot=(2, 11), ag_h2=(2, 11), ag_gb=(2, 11),
    rs_r2=(2, 10), rs_ro=(2, 10), rs_r1=(2, 10),
    sm=(2, 16), sm_back=(32,), sm_fwd=(2,),
    sa=(2, 16), sa_back=(32,), sa_fwd=(2,),
    g1=(4, 16), g2=(4, 16),
    sw_x=(3,), sw_cot=(3,), sw_lo=(3,), sw_tg=(3,),
    f_w=(5,), f_wo=(5,), f_wg=(5,), f_wm=(5,),
    x_o=(2, 8), x_do=(2, 8), outs=(4,),
)


def kernel(
    tok, cot, win, wout, wgate, wmix, gain1, gain2, cosine, signed,
    lo_ref, tg_ref, gm_ref, ga_ref, gains_ref, *scratch
):
    names = list(SCRATCH) + ["s_" + n for n in SEMS]
    s = dict(zip(names, scratch, strict=True))
    p = Place()

    class R:
        pass

    r = R()
    r.__dict__.update(s)

    barrier = pltpu.get_barrier_semaphore()

    @pl.loop(1, 8)
    def _(k):
        j = (p.me + k) % 8
        pl.semaphore_signal(barrier, inc=1, device_id=p.team(j % 2, j // 2), device_id_type=MESH)

    @pl.loop(1, 16)
    def _(k):
        dev = p.plane((p.x + k % 4) % 4, (p.z + k // 4) % 4)
        pl.semaphore_signal(barrier, inc=1, device_id=dev, device_id_type=MESH)

    for d in (1, 3):
        dev = p.plane((p.x + d) % 4, p.z, 1 - p.c)
        pl.semaphore_signal(barrier, inc=1, device_id=dev, device_id_type=MESH)
    pl.semaphore_wait(barrier, 24)

    def gather(buf, name):
        sem = s["s_ag_" + name]
        return Gather(p, buf, sem.at[0], sem.at[1])

    def scatter(name):
        parts = [s[name + "_" + n] for n in ("part", "got", "held", "top", "bottom", "left", "right")]
        sem = s["s_rs_" + name]
        return Scatter(p, *parts, sem.at[0], sem.at[1])

    own = rows(p.me * B, B)
    other = rows((2 * p.y + 1 - p.c) * B, B)
    own_cols = cols(p.me * B, B)

    sw_x = Swap(p, tok, r.xb, r.s_sw_x)
    f_w = Fetch(p, win, r.w, (pl.ds(0, 512), pl.ds(512, 512)), r.s_f_w)
    sw_x.start()
    f_w.start()
    sw_x.wait()

    xhat, inverse = norm(r.xb[...].astype(F32))
    r.xhat1[...] = xhat
    r.inv1[...] = inverse
    r.h1[own, :] = (xhat * gain1[...]).astype(BF)
    ag_h1 = gather(r.h1, "h1")
    ag_h1.start()

    f_wo = Fetch(p, wout, r.wo.at[own], (pl.ds(0, 64), pl.ds(64, 64)), r.s_f_wo, r.wo.at[other])
    sw_cot = Swap(p, cot, r.cotb.at[own], r.s_sw_cot, r.cotb.at[other])
    f_wo.start()
    sw_cot.start()
    r.qt[...] = jnp.zeros_like(r.qt)
    f_w.wait()

    def project(yy):
        at = rows(yy * 256, 256)
        lanes = cols(yy * 256, 256)
        u = nn(r.h1[at, :], r.w[...])
        co, si = cosine[at, :], signed[at, :]
        q = u[:, :128]
        q = (q * co + swap_halves(q) * si).astype(BF).astype(F32) * 0.125
        r.q[at, :] = q.astype(BF)
        qt = q.T.astype(BF)
        r.qt[0, 0:64, lanes] = qt[0:64]
        r.qt[1, 64:128, lanes] = qt[64:128]
        k = u[:, 128:256]
        k = k * co + swap_halves(k) * si
        r.k[at, :] = k.astype(BF)
        r.kt[:, lanes] = k.T.astype(BF)
        v = u[:, 256:]
        r.v[at, :] = v.astype(BF)
        r.vt[:, lanes] = v.T.astype(BF)

    ag_h1.steps(project)
    f_wg = Fetch(p, wgate, r.wg, (0, 1), r.s_f_wg)
    f_wm = Fetch(p, wmix, r.wm, (pl.ds(0, 192), pl.ds(192, 192)), r.s_f_wm)
    f_wg.start()
    f_wm.start()
    ag_wo = gather(r.wo, "wo")
    ag_cot = gather(r.cotb, "cot")
    f_wo.wait()
    ag_wo.start()

    @pl.loop(0, 8)
    def _(it):
        h, part = it // 4, it % 4
        lanes = cols(part * 256, 256)

        @pl.when(it == 2)
        def _():
            ag_wo.first()
            ag_wo.second()

        @pl.when(it == 4)
        def _():
            ag_wo.third()

        scores = nn(r.k[...], r.qt[h, :, lanes])
        powers = jnp.exp(scores - jnp.max(scores, 0, keepdims=True))
        probs = (powers * (1.0 / jnp.sum(powers, 0, keepdims=True))).astype(BF)
        r.pt[h, :, lanes] = probs
        half = rows(h * 64, 64)
        r.ot[half, lanes] = nn(r.vt[half, :], probs)

    r.o[...] = r.ot[...].T.astype(BF)
    x_o = Exchange(
        p, lambda j: r.o.at[rows(j * B, B)], r.orow.at[:, own_cols], r.s_x_o.at[0], r.s_x_o.at[1]
    )
    x_o.start()
    r.orow[:, own_cols] = r.o[own, :]
    ag_wo.rest()
    sw_cot.wait()
    ag_cot.start()
    x_o.wait()

    y1 = r.xb[...].astype(F32) + nn(r.orow[...], r.wo[...])
    r.y1[...] = y1
    xhat, inverse = norm(y1)
    r.xhat2[...] = xhat
    r.inv2[...] = inverse
    r.h2[own, :] = (xhat * gain2[...]).astype(BF)
    ag_h2 = gather(r.h2, "h2")
    ag_cot.first()
    ag_cot.second()
    ag_h2.start()
    ag_cot.third()
    ag_cot.rest()
    f_wg.wait()
    f_wm.wait()

    def mix(yy):
        at = rows(yy * 256, 256)
        lanes = cols(yy * 256, 256)
        h2 = r.h2[at, :]
        a = nn(h2, r.wg[0])
        b = nn(h2, r.wg[1])
        cdf = 0.5 * (1.0 + lax.erf(a * 0.7071067811865476))
        gelu = a * cdf
        slope = cdf + a * (jnp.exp(-0.5 * a * a) * 0.3989422804014327)
        m = gelu * b
        dm = nt(r.cotb[at, :], r.wm[...]).astype(BF).astype(F32)
        da = dm * b * slope
        db = dm * gelu
        r.m[at, :] = m.astype(BF)
        r.da[at, :] = da.astype(BF)
        r.db[at, :] = db.astype(BF)
        r.mt[:, lanes] = m.T.astype(BF)
        r.dat[:, lanes] = da.T.astype(BF)
        r.dbt[:, lanes] = db.T.astype(BF)

    ag_h2.steps(mix)

    def back_mix(yy):
        at = rows(yy * 256, 256)
        return nt(r.da[at, :], r.wg[0]) + nt(r.db[at, :], r.wg[1])

    rs_2 = scatter("r2")
    rs_2.phase(back_mix)
    rs_2.step0()

    def weight_grad(out, first, lhs, size, rhs):
        @pl.loop(0, 4)
        def _(i):
            lanes = cols(i * 256, 256)
            out[first : first + size, lanes] = nn(lhs[0:size, :], rhs[:, lanes]).astype(BF)

    weight_grad(r.gm, 0, r.mt, FR, r.cotb)
    rs_2.step1()
    weight_grad(r.gm, FR, r.dat, FR, r.h2)
    weight_grad(r.gm, 2 * FR, r.dbt, FR, r.h2)
    r.gm[3 * FR :, :] = jnp.zeros((1024 - 3 * FR, D), BF)
    dh2 = rs_2.step2()

    dx, dgain2 = norm_back(dh2, r.xhat2[...], r.inv2[...], gain2[...])
    gy = r.cotb[own, :].astype(F32) + dx
    r.gy[...] = gy
    r.gb[own, :] = gy.astype(BF)
    r.dorow[...] = nt(r.gb[own, :], r.wo[...]).astype(BF)
    x_do = Exchange(
        p, lambda j: r.dorow.at[:, cols(j * B, B)], r.dob.at[own], r.s_x_do.at[0], r.s_x_do.at[1]
    )
    x_do.start()
    r.dob[own, :] = r.dorow[:, own_cols]
    gain_2 = Gain(p, r.g2t, r.g2p, r.s_g2)
    gain_2.start(dgain2)
    sums_m = Sums(
        p, r.gm, r.gm_slots, r.gm_mine, r.gm_out, 64, r.s_sm.at[0], r.s_sm.at[1], r.s_sm_back, r.s_sm_fwd
    )
    sums_m.spread()
    rs_o = scatter("ro")
    rs_o.phase(lambda yy: nn(r.m[rows(yy * 256, 256), :], r.wm[...]))
    x_do.wait()
    ag_gb = gather(r.gb, "gb")
    ag_gb.start()
    rs_o.step0()

    dot = r.dob[...].astype(F32).T
    r.dot[...] = jnp.zeros_like(r.dot)
    r.dot[0, 0:64, :] = dot[0:64].astype(BF)
    r.dot[1, 64:128, :] = dot[64:128].astype(BF)
    prod = dot * r.ot[...]
    r.dsum[0] = jnp.sum(prod[0:64], 0, keepdims=True)
    r.dsum[1] = jnp.sum(prod[64:128], 0, keepdims=True)

    @pl.loop(0, 8)
    def _(it):
        h, part = it // 4, it % 4
        lanes = cols(part * 256, 256)

        @pl.when(it == 2)
        def _():
            rs_o.step1()
            gain_2.middle()

        @pl.when(it == 4)
        def _():
            ag_gb.first()
            ag_gb.second()

        @pl.when(it == 6)
        def _():
            ag_gb.third()

        dp = nn(r.v[...], r.dot[h, :, lanes])
        ds = (r.pt[h, :, lanes].astype(F32) * (dp - r.dsum[h, :, lanes])).astype(BF)
        r.ds[:, lanes] = ds
        half = rows(h * 64, 64)
        r.dqt[half, lanes] = nn(r.kt[half, :], ds)

        @pl.when(part == 3)
        def _():
            @pl.loop(0, 4)
            def _(i):
                at = rows(i * 256, 256)
                lane = lax.broadcasted_iota(jnp.int32, (256, B), 1)
                keep = (lane // 64) == h
                r.dk[at, :] = jnp.where(keep, nn(r.ds[at, :], r.q[...]), r.dk[at, :])
                r.dv[at, :] = jnp.where(keep, nn(r.pt[h, at, :], r.dob[...]), r.dv[at, :])

    @pl.loop(0, 4)
    def _(i):
        at = rows(i * 256, 256)
        lanes = cols(i * 256, 256)
        co, si = cosine[at, :], signed[at, :]
        dq = r.dqt[:, lanes].T * 0.125
        dq = dq * co - swap_halves(dq) * si
        dk = r.dk[at, :]
        dk = dk * co - swap_halves(dk) * si
        dv = r.dv[at, :]
        r.dqkv[at, 0:128] = dq.astype(BF)
        r.dqkv[at, 128:256] = dk.astype(BF)
        r.dqkv[at, 256:384] = dv.astype(BF)
        r.dqkvt[0:128, lanes] = dq.T.astype(BF)
        r.dqkvt[128:256, lanes] = dk.T.astype(BF)
        r.dqkvt[256:384, lanes] = dv.T.astype(BF)

    rs_1 = scatter("r1")
    rs_1.phase(lambda yy: nt(r.dqkv[rows(yy * 256, 256), :], r.w[...]))
    rs_1.step0()
    weight_grad(r.ga, 0, r.dqkvt, 384, r.h1)
    ag_gb.rest()

    @pl.loop(0, 4)
    def _(i):
        lanes = cols(i * 256, 256)
        r.ga[384:512, lanes] = nn(r.ot[...].astype(BF), r.gb[:, lanes]).astype(BF)

    sums_a = Sums(
        p, r.ga, r.ga_slots, r.ga_mine, r.ga_out, 32, r.s_sa.at[0], r.s_sa.at[1], r.s_sa_back, r.s_sa_fwd
    )
    sums_a.spread()
    rs_1.step1()
    sums_m.add()
    sums_m.give()
    r.lo_here[...] = (r.y1[...] + rs_o.step2()).astype(BF)
    sw_lo = Swap(p, r.lo_here, r.lo_out, r.s_sw_lo)
    sw_lo.start()
    dh1 = rs_1.step2()
    dx, dgain1 = norm_back(dh1, r.xhat1[...], r.inv1[...], gain1[...])
    gain_1 = Gain(p, r.g1t, r.g1p, r.s_g1)
    gain_1.start(dgain1)
    r.tg_here[...] = (r.gy[...] + dx).astype(BF)
    sw_tg = Swap(p, r.tg_here, r.tg_out, r.s_sw_tg)
    sw_tg.start()
    sums_a.add()
    sums_a.give()
    gain_1.middle()
    sums_m.take()
    sw_lo.wait()
    lo_copy = pltpu.make_async_copy(r.lo_out, lo_ref, r.s_outs.at[0])
    lo_copy.start()
    sw_tg.wait()
    tg_copy = pltpu.make_async_copy(r.tg_out, tg_ref, r.s_outs.at[1])
    tg_copy.start()
    gains_ref[1:2, :] = gain_2.end()
    sums_m.finish()
    gm_copy = pltpu.make_async_copy(r.gm_out, gm_ref, r.s_outs.at[2])
    gm_copy.start()
    gains_ref[0:1, :] = gain_1.end()
    sums_a.take()
    sums_a.finish()
    ga_copy = pltpu.make_async_copy(r.ga_out, ga_ref, r.s_outs.at[3])
    ga_copy.start()
    lo_copy.wait()
    tg_copy.wait()
    gm_copy.wait()
    ga_copy.wait()


def local(tokens, attn_in, attn_out, mlp_in, mlp_out, norm_first, norm_second, cotangent):
    cosine, signed = tables()
    any_space = pl.BlockSpec(memory_space=pl.ANY)
    vmem = pl.BlockSpec(memory_space=pltpu.VMEM)
    lo, tg, gm, ga, gains = pl.pallas_call(
        kernel,
        out_shape=(
            jax.ShapeDtypeStruct((B, D), BF),
            jax.ShapeDtypeStruct((B, D), BF),
            jax.ShapeDtypeStruct((1024, D), BF),
            jax.ShapeDtypeStruct((512, D), BF),
            jax.ShapeDtypeStruct((2, D), F32),
        ),
        in_specs=[any_space] * 6 + [vmem] * 4,
        out_specs=(any_space, any_space, any_space, any_space, vmem),
        scratch_shapes=[pltpu.VMEM(shape, kind) for shape, kind in SCRATCH.values()]
        + [pltpu.SemaphoreType.DMA(shape) for shape in SEMS.values()],
        compiler_params=pltpu.CompilerParams(
            collective_id=0, has_side_effects=True, vmem_limit_bytes=63 * 1024 * 1024
        ),
    )(
        tokens,
        cotangent,
        attn_in.reshape(D, 384),
        attn_out.reshape(B, D),
        jnp.pad(mlp_in, ((0, 0), (0, 0), (0, FP - FF))),
        jnp.pad(mlp_out, ((0, FP - FF), (0, 0))),
        norm_first.reshape(1, D),
        norm_second.reshape(1, D),
        jnp.asarray(cosine),
        jnp.asarray(signed),
    )
    attn_in_grad = ga[:384].astype(F32).T.reshape(D, 3, 2, 64)
    attn_out_grad = ga[384:].astype(F32).reshape(2, 64, D)
    mlp_out_grad = gm[:FF].astype(F32)
    mlp_in_grad = jnp.stack(
        [gm[FR : FR + FF].astype(F32).T, gm[2 * FR : 2 * FR + FF].astype(F32).T]
    )
    return (
        lo,
        tg.astype(F32),
        attn_in_grad,
        attn_out_grad,
        mlp_in_grad,
        mlp_out_grad,
        gains[0],
        gains[1],
    )


def solution(mesh):
    placed = (
        P(("dp", "tensor"), None),
        P(None, None, "tensor", None),
        P("tensor", None, None),
        P(None, None, "tensor"),
        P("tensor", None),
        P(),
        P(),
        P(("dp", "tensor"), None),
    )
    return jax.shard_map(
        local,
        mesh=mesh,
        in_specs=placed,
        out_specs=(
            P(("dp", "tensor"), None),
            P(("dp", "tensor"), None),
            P(None, None, "tensor", None),
            P("tensor", None, None),
            P(None, None, "tensor"),
            P("tensor", None),
            P(),
            P(),
        ),
        check_vma=False,
    )
```

```python
import jax
import jax.numpy as jnp
import numpy as np
from jax import lax
from jax.experimental import pallas as pl
from jax.experimental.pallas import tpu as pltpu
from jax.sharding import PartitionSpec as P

MESH = pl.DeviceIdType.MESH
BF = jnp.bfloat16
F32 = jnp.float32
EPS = 1e-05
THETA = 160000.0
T = 1024
D = 1024
B = 128
FF = 328
FR = 336
LOG2E = 1.4426950408889634


def tables():
    places = np.arange(T, dtype=np.float32)
    frequency = (THETA ** (-np.arange(0, 64, 2, dtype=np.float32) / 64)).astype(np.float32)
    angles = places[:, None] * frequency[None, :]
    cosine, sine = np.cos(angles), np.sin(angles)
    cosine = np.concatenate([cosine, cosine] * 2, -1)
    signed = np.concatenate([-sine, sine] * 2, -1)
    order = np.concatenate([np.arange(B) + ((j % 2) * 4 + j // 2) * B for j in range(8)])
    return cosine[order].astype(np.float32), signed[order].astype(np.float32)


def nn(a, b):
    return jnp.dot(a, b, preferred_element_type=F32)


def nt(a, b):
    return lax.dot_general(a, b, (((1,), (1,)), ((), ())), preferred_element_type=F32)


def pick(step, a, b, c, d):
    return jnp.where(step == 0, a, jnp.where(step == 1, b, jnp.where(step == 2, c, d)))


def swap_halves(u):
    lane = lax.broadcasted_iota(jnp.int32, u.shape, 1)
    return jnp.where((lane % 64) < 32, pltpu.roll(u, 96, 1), pltpu.roll(u, 32, 1))


def norm(v):
    centred = v - jnp.mean(v, -1, keepdims=True)
    inverse = lax.rsqrt(jnp.mean(centred * centred, -1, keepdims=True) + EPS)
    return centred * inverse, inverse


def norm_back(gradient, xhat, inverse, gain):
    e = gradient * gain
    dx = inverse * (
        e - jnp.mean(e, -1, keepdims=True) - xhat * jnp.mean(e * xhat, -1, keepdims=True)
    )
    return dx, jnp.sum(gradient * xhat, 0, keepdims=True)


def rows(start, size):
    return pl.ds(pl.multiple_of(start, 16), size)


def cols(start, size):
    return pl.ds(pl.multiple_of(start, 128), size)


def remote(src, dst, ssem, rsem, dev):
    return pltpu.make_async_remote_copy(
        src_ref=src, dst_ref=dst, send_sem=ssem, recv_sem=rsem, device_id=dev, device_id_type=MESH
    )


def drain(ref, sem):
    pltpu.make_async_copy(ref, ref, sem).wait()


class Place:
    def __init__(self):
        dp, tensor = lax.axis_index("dp"), lax.axis_index("tensor")
        self.dp, self.tensor = dp, tensor
        self.c = dp % 2
        self.xlo, self.y = tensor // 4, tensor % 4
        self.z = dp // 4
        self.x = ((dp // 2) % 2) * 2 + self.xlo
        self.me = 2 * self.y + self.c
        self.mover = self.c != self.xlo
        self.right, self.left = (self.y + 1) % 4, (self.y + 3) % 4
        self.opp = (self.y + 2) % 4

    def team(self, core, y):
        return {"dp": self.dp - self.c + core, "tensor": self.xlo * 4 + y}

    def plane(self, x, z, core=None):
        core = self.c if core is None else core
        return {"dp": z * 4 + (x // 2) * 2 + core, "tensor": (x % 2) * 4 + self.y}

    def partner(self):
        return {"dp": self.dp - self.c + self.xlo, "tensor": self.c * 4 + self.y}


class Gather:
    def __init__(self, place, buf, sems):
        self.p, self.buf, self.sems = place, buf, sems

    def msg(self, i):
        p = self.p
        me, lt, rt, op = p.me, 2 * p.left + p.c, 2 * p.right + p.c, 2 * p.opp + p.c
        right, left = p.team(p.c, p.right), p.team(p.c, p.left)
        sib = p.team(1 - p.c, p.y)
        block, first, size, dev = (
            (me, 0, 64, right),
            (me, 64, 64, left),
            (me, 64, 64, right),
            (me, 0, 64, left),
            (me, 0, 128, sib),
            (lt, 0, 64, right),
            (rt, 64, 64, left),
            (lt, 0, 128, sib),
            (rt, 0, 128, sib),
            (op, 0, 64, sib),
            (op, 64, 64, sib),
        )[i]
        ref = self.buf.at[rows(block * B + first, size)]
        return remote(ref, ref, self.sems.at[11], self.sems.at[i], dev)

    def start(self):
        for i in range(5):
            self.msg(i).start()

    def start_top(self):
        self.msg(0).start()
        self.msg(3).start()

    def start_bottom(self):
        self.msg(1).start()
        self.msg(2).start()
        self.msg(4).start()

    def first(self):
        self.msg(4).wait_recv()

    def second(self):
        self.msg(0).wait_recv()
        self.msg(5).start()
        self.msg(1).wait_recv()
        self.msg(6).start()
        self.msg(2).wait_recv()
        self.msg(7).start()
        self.msg(3).wait_recv()
        self.msg(8).start()

    def third(self):
        self.msg(5).wait_recv()
        self.msg(9).start()
        self.msg(6).wait_recv()
        self.msg(10).start()

    def left_in(self):
        self.msg(7).wait_recv()

    def right_in(self):
        self.msg(8).wait_recv()

    def opp_in(self):
        self.msg(9).wait_recv()
        self.msg(10).wait_recv()

    def sent(self):
        drain(self.buf.at[pl.ds(0, 896)], self.sems.at[11])

    def rest(self):
        self.left_in()
        self.right_in()
        self.opp_in()
        self.sent()

    def steps(self, body, hook=None, forwarded=False):
        p = self.p

        @pl.loop(0, 4)
        def _(step):
            @pl.when(step == 0)
            def _():
                self.first()

            @pl.when(step == 1)
            def _():
                if not forwarded:
                    self.second()
                self.left_in()

            @pl.when(step == 2)
            def _():
                self.right_in()

            @pl.when(step == 3)
            def _():
                self.third()
                self.opp_in()

            if hook is not None:
                hook(step)
            body((p.y + pick(step, 0, 3, 1, 2)) % 4)

        self.sent()


class Scatter:
    def __init__(self, place, part, got, held, top, bottom, from_left, from_right, sems):
        self.p = place
        self.part, self.got, self.held = part, got, held
        self.top, self.bottom = top, bottom
        self.from_left, self.from_right = from_left, from_right
        self.sems = sems

    def off(self, step):
        return pick(step, 2, 1, 3, 0)

    def sib(self, step):
        p = self.p
        yy = (p.y + self.off(step)) % 4
        return remote(
            self.part.at[rows((2 * yy + 1 - p.c) * B, B)],
            self.got.at[rows(yy * B, B)],
            self.sems.at[10],
            self.sems.at[step],
            p.team(1 - p.c, p.y),
        )

    def msg(self, i):
        p = self.p
        right, left = p.team(p.c, p.right), p.team(p.c, p.left)
        block, first, dst, dev = (
            (p.opp, 0, self.top, right),
            (p.opp, 64, self.bottom, left),
            (p.right, 64, self.from_left.at[rows(64, 64)], right),
            (p.right, 0, self.from_left.at[rows(0, 64)], right),
            (p.left, 0, self.from_right.at[rows(0, 64)], left),
            (p.left, 64, self.from_right.at[rows(64, 64)], left),
        )[i]
        return remote(
            self.held.at[rows(block * B + first, 64)], dst, self.sems.at[10], self.sems.at[4 + i], dev
        )

    def phase(self, compute, early=True, hook=None):
        p = self.p

        @pl.loop(0, 4)
        def _(step):
            yy = (p.y + self.off(step)) % 4
            self.part[rows(yy * 256, 256), :] = compute(yy).astype(BF)
            self.sib(step).start()
            if early:
                pl.when(step == 1)(self.step0)
                pl.when(step == 2)(self.step_right)
                pl.when(step == 3)(self.step_left)
            if hook is not None:
                hook(step)

    def pair_sum(self, yy):
        own = self.part[rows((2 * yy + self.p.c) * B, B), :].astype(F32)
        return own + self.got[rows(yy * B, B), :].astype(F32)

    def step0(self):
        p = self.p
        self.sib(0).wait_recv()
        self.held[rows(p.opp * B, B), :] = self.pair_sum(p.opp).astype(BF)
        self.msg(0).start()
        self.msg(1).start()

    def step_right(self):
        p = self.p
        self.sib(1).wait_recv()
        self.held[rows(p.right * B, B), :] = self.pair_sum(p.right).astype(BF)
        self.msg(2).start()

    def step_left(self):
        p = self.p
        self.sib(2).wait_recv()
        self.held[rows(p.left * B, B), :] = self.pair_sum(p.left).astype(BF)
        self.msg(4).start()

    def step1(self):
        p = self.p
        top, bottom = rows(p.right * B, 64), rows(p.left * B + 64, 64)
        self.msg(0).wait_recv()
        self.held[top, :] = (self.held[top, :].astype(F32) + self.top[...].astype(F32)).astype(BF)
        self.msg(3).start()
        self.msg(1).wait_recv()
        self.held[bottom, :] = (
            self.held[bottom, :].astype(F32) + self.bottom[...].astype(F32)
        ).astype(BF)
        self.msg(5).start()

    def step2(self):
        p = self.p
        self.sib(3).wait_recv()
        total = self.pair_sum(p.y)
        for i in range(2, 6):
            self.msg(i).wait_recv()
        total = total + self.from_left[...].astype(F32) + self.from_right[...].astype(F32)
        drain(self.part.at[pl.ds(0, 896)], self.sems.at[10])
        return total


class Sums:
    def __init__(self, place, full, slots, mine, out, sems):
        self.p = place
        self.full, self.slots, self.mine, self.out = full, slots, mine, out
        self.size = full.shape[0] // 2
        self.sems = sems

    def peer(self, k):
        return (self.p.x + k % 4) % 4, (self.p.z + k // 4) % 4

    def chunk(self, x, z):
        return rows((x % 2) * self.size, self.size), cols((z * 2 + x // 2) * B, B)

    def spread_msg(self, k):
        x, z = self.peer(k)
        return remote(
            self.full.at[self.chunk(x, z)],
            self.slots.at[k],
            self.sems.at[0],
            self.sems.at[1],
            self.p.plane(x, z),
        )

    def spread(self, off):
        @pl.loop(0, 4)
        def _(i):
            k = off * 4 + i

            @pl.when(k != 0)
            def _():
                self.spread_msg(k).start()

    def add(self):
        p, size = self.p, self.size

        drain(self.slots.at[pl.ds(1, 15)], self.sems.at[1])
        own_cols = cols((p.z * 2 + p.x // 2) * B, B)

        @pl.loop(0, size // 64)
        def _(r):
            total = self.full[rows((p.x % 2) * size + r * 64, 64), own_cols].astype(F32)
            for k in range(1, 16):
                total = total + self.slots[k, rows(r * 64, 64), :].astype(F32)
            self.mine[rows(r * 64, 64), :] = total.astype(BF)

    def return_msg(self, k):
        p = self.p
        x, z = self.peer(k)
        return remote(
            self.mine,
            self.out.at[self.chunk(p.x, p.z)],
            self.sems.at[2],
            self.sems.at[4 + k // 4],
            p.plane(x, z),
        )

    def goes(self, k):
        return ((self.p.x + k % 4) % 2 == self.p.c) & (k != 0)

    def give(self):
        p = self.p

        @pl.loop(0, 16)
        def _(k):
            @pl.when(self.goes(k))
            def _():
                self.return_msg(k).start()

        @pl.when(jnp.logical_not(p.mover))
        def _():
            at, lanes = self.chunk(p.x, p.z)
            self.out[at, lanes] = self.mine[...]

    def forward(self, i):
        p = self.p
        block = self.out.at[:, cols(((p.z + 4 - i) % 4) * 256, 256)]
        return remote(block, block, self.sems.at[3], self.sems.at[8 + i], p.team(1 - p.c, p.y))

    def take(self):
        p = self.p

        @pl.when(jnp.logical_not(p.mover))
        def _():
            for i in range(4):
                drain(self.slots.at[pl.ds(0, 4 if i else 3)], self.sems.at[4 + i])
                self.forward(i).start()

    def finish(self):
        p = self.p

        @pl.when(p.mover)
        def _():
            @pl.loop(0, 4)
            def _(i):
                self.forward(i).wait_recv()

            drain(self.slots.at[pl.ds(0, 8)], self.sems.at[2])

        @pl.when(jnp.logical_not(p.mover))
        def _():
            drain(self.out, self.sems.at[3])
            drain(self.slots.at[pl.ds(0, 7)], self.sems.at[2])

        drain(self.slots.at[pl.ds(1, 15)], self.sems.at[0])


class Gain:
    def __init__(self, place, team_buf, plane_buf, sems):
        self.p, self.team_buf, self.plane_buf, self.sems = place, team_buf, plane_buf, sems

    def start(self, value):
        p = self.p
        ref = self.team_buf.at[p.me]
        ref[...] = value

        @pl.loop(1, 8)
        def _(k):
            j = (p.me + k) % 8
            remote(ref, ref, self.sems.at[0], self.sems.at[1], p.team(j % 2, j // 2)).start()

    def middle(self):
        p = self.p
        drain(self.team_buf.at[pl.ds(0, 7)], self.sems.at[1])
        ref = self.plane_buf.at[p.z * 4 + p.x]
        ref[...] = jnp.sum(self.team_buf[...], 0)

        @pl.loop(1, 16)
        def _(k):
            dev = p.plane((p.x + k % 4) % 4, (p.z + k // 4) % 4)
            remote(ref, ref, self.sems.at[2], self.sems.at[3], dev).start()

        drain(self.team_buf.at[pl.ds(0, 7)], self.sems.at[0])

    def end(self):
        drain(self.plane_buf.at[pl.ds(0, 15)], self.sems.at[3])
        total = jnp.sum(self.plane_buf[...], 0)
        drain(self.plane_buf.at[pl.ds(0, 15)], self.sems.at[2])
        return total


class Swap:
    def __init__(self, place, src, dst, sems, there=None):
        self.p, self.src, self.dst, self.sems = place, src, dst, sems
        self.there = dst if there is None else there

    def far(self):
        return remote(self.src, self.there, self.sems.at[0], self.sems.at[1], self.p.partner())

    def near(self):
        return pltpu.make_async_copy(self.src, self.dst, self.sems.at[2])

    def start(self):
        self.start_far()
        self.start_near()

    def start_far(self):
        pl.when(self.p.mover)(lambda: self.far().start())

    def start_near(self):
        pl.when(jnp.logical_not(self.p.mover))(lambda: self.near().start())

    def wait(self):
        pl.when(self.p.mover)(lambda: self.far().wait())
        pl.when(jnp.logical_not(self.p.mover))(lambda: self.near().wait())


class Fetch:
    def __init__(self, place, src, dst, part, sems):
        self.p, self.src, self.dst, self.part, self.sems = place, src, dst, part, sems

    def far(self, role):
        p = self.p
        step = 1 + 2 * ((p.x + role) % 2)
        part = self.part(role)
        return remote(
            self.src.at[part],
            self.dst.at[part],
            self.sems.at[role],
            self.sems.at[2 + role],
            p.plane((p.x + step) % 4, p.z, p.xlo),
        )

    def near(self):
        return pltpu.make_async_copy(self.src, self.dst, self.sems.at[4])

    def start(self):
        self.start_away()
        self.start_partner()

    def start_away(self):
        pl.when(self.p.mover)(lambda: self.far(1).start())
        pl.when(jnp.logical_not(self.p.mover))(lambda: self.near().start())

    def start_partner(self):
        pl.when(self.p.mover)(lambda: self.far(0).start())

    def wait(self):
        @pl.when(self.p.mover)
        def _():
            self.far(0).wait()
            self.far(1).wait()

        pl.when(jnp.logical_not(self.p.mover))(lambda: self.near().wait())


class WholeWeight:
    def __init__(self, place, src, buf, sems):
        self.p, self.src, self.buf, self.sems = place, src, buf, sems

    def near(self):
        p = self.p
        return pltpu.make_async_copy(
            self.src, self.buf.at[rows((2 * p.y + p.xlo) * B, B)], self.sems.at[18]
        )

    def msg(self, i):
        p = self.p
        right, left = p.team(p.c, p.right), p.team(p.c, p.left)
        sib = p.team(1 - p.c, p.y)
        side = p.plane((p.x + 1 + 2 * p.c) % 4, p.z)
        ys = (p.y, p.left, p.right, p.opp)
        first, size = 0, 64
        if i < 6:
            y, first, size, dev = (
                (p.y, 0, 32, right),
                (p.y, 32, 32, left),
                (p.y, 32, 32, right),
                (p.y, 0, 32, left),
                (p.left, 0, 32, right),
                (p.right, 32, 32, left),
            )[i]
            group = p.xlo
        elif i < 10:
            y, group, dev = ys[i - 6], p.xlo, side
        elif i < 13:
            y, group, dev = ys[i - 9], p.xlo, sib
        else:
            y, group, dev = ys[i - 13], 1 - p.xlo, sib
        ref = self.buf.at[rows((2 * y + group) * B + p.c * 64 + first, size)]
        return remote(ref, ref, self.sems.at[17], self.sems.at[i], dev)

    def go(self, *which):
        for i in which:
            self.msg(i).start()

    def got(self, *which):
        for i in which:
            self.msg(i).wait_recv()

    def w0(self):
        self.near().wait()
        self.go(0, 1, 2, 3)

    def w1(self):
        self.go(6)
        self.got(0)
        self.go(4)
        self.got(1)
        self.go(5)
        self.got(2)
        self.go(7, 10)
        self.got(3)
        self.go(8, 11)

    def w2(self):
        self.got(4, 5)
        self.go(9, 12)

    def w3(self):
        for i in range(4):
            self.got(6 + i)
            self.go(13 + i)

    def w4(self):
        self.got(*range(10, 17))
        drain(self.buf.at[pl.ds(0, 896)], self.sems.at[17])


class Ring:
    def __init__(self, i, right, left, blk, bufs, sems):
        self.i, self.right, self.left, self.blk = i, right, left, blk
        self.bufs, self.sems = bufs, sems

    def msg(self, k):
        i, blk, bufs = self.i, self.blk, self.bufs
        src, slot, dev = (
            (lambda: blk((i + 2) % 4, 0), 0, self.right),
            (lambda: blk((i + 2) % 4, 1), 1, self.left),
            (lambda: blk((i + 1) % 4, 1), 5, self.right),
            (lambda: bufs.at[2], 4, self.right),
            (lambda: blk((i + 3) % 4, 0), 6, self.left),
            (lambda: bufs.at[3], 7, self.left),
        )[k]
        return remote(src(), bufs.at[slot], self.sems.at[6], self.sems.at[k], dev)

    def s0(self):
        for k in (0, 1, 2, 4):
            self.msg(k).start()

    def s1(self):
        bufs = self.bufs
        self.msg(0).wait_recv()
        bufs[2] = (self.blk((self.i + 1) % 4, 0)[...].astype(F32) + bufs[0].astype(F32)).astype(BF)
        self.msg(3).start()
        self.msg(1).wait_recv()
        bufs[3] = (self.blk((self.i + 3) % 4, 1)[...].astype(F32) + bufs[1].astype(F32)).astype(BF)
        self.msg(5).start()

    def s2(self, store):
        bufs = self.bufs
        for k in range(2, 6):
            self.msg(k).wait_recv()
        for h in range(2):
            total = self.blk(self.i, h)[...].astype(F32)
            total = total + bufs[4 + h].astype(F32) + bufs[6 + h].astype(F32)
            store(h, total.astype(BF))

    def sent(self):
        drain(self.bufs.at[pl.ds(0, 6)], self.sems.at[6])


class PlaneSum:
    def __init__(self, place, full, big, res, small, mine, out, sems, back, spare):
        p = self.p = place
        self.full, self.mine, self.out, self.back, self.res = full, mine, out, back, res
        self.sends = spare
        half = pl.ds(0, 512), pl.ds(512, 512)
        along_z = p.z, p.plane(p.x, (p.z + 1) % 4), p.plane(p.x, (p.z + 3) % 4)
        along_x = p.x, p.plane((p.x + 1) % 4, p.z), p.plane((p.x + 3) % 4, p.z)
        self.first = (
            Ring(
                *along_z, lambda j, h: full.at[j, pl.ds(2 * h, 2), :, half[0]],
                big.at[0], sems.at[0],
            ),
            Ring(
                *along_x, lambda j, h: full.at[pl.ds(2 * h, 2), j, :, half[1]],
                big.at[1], sems.at[1],
            ),
        )
        self.second = tuple(
            Ring(
                *along, lambda j, h, n=n: res.at[n, j, :, pl.ds(h * 256, 256)],
                small.at[n], sems.at[2 + n],
            )
            for n, along in enumerate((along_x, along_z))
        )

    def to_second(self):
        for n in range(2):

            def store(h, value, n=n):
                self.res[n, 2 * h : 2 * h + 2] = value

            self.first[n].s2(store)
            self.second[n].s0()

    def to_mine(self):
        for n in range(2):

            def store(h, value, n=n):
                self.mine[:, n * 512 + h * 256 : n * 512 + h * 256 + 256] = value

            self.second[n].s2(store)

    def side(self, i):
        p = self.p
        return remote(
            self.mine,
            self.out.at[p.z, p.x],
            self.back.at[15],
            self.back.at[11 + i],
            p.plane((p.x + (1, 3, 2)[i]) % 4, p.z),
        )

    def msg(self, i):
        p = self.p
        lt, rt, op = (p.z + 3) % 4, (p.z + 1) % 4, (p.z + 2) % 4
        right, left, sib = p.plane(p.x, rt), p.plane(p.x, lt), p.team(1 - p.c, p.y)
        block, first, size, dev = (
            (p.z, 0, 2, right),
            (p.z, 2, 2, left),
            (p.z, 2, 2, right),
            (p.z, 0, 2, left),
            (p.z, 0, 4, sib),
            (lt, 0, 2, right),
            (rt, 2, 2, left),
            (lt, 0, 4, sib),
            (rt, 0, 4, sib),
            (op, 0, 2, sib),
            (op, 2, 2, sib),
        )[i]
        ref = self.out.at[block, pl.ds(first, size)]
        return remote(ref, ref, self.back.at[14], self.back.at[i], dev)

    def g0(self):
        p = self.p

        @pl.when(p.mover)
        def _():
            self.side(0).start()
            self.side(1).start()

        @pl.when(jnp.logical_not(p.mover))
        def _():
            self.side(2).start()
            self.out[p.z, p.x] = self.mine[...]

    def stays(self, body):
        pl.when(jnp.logical_not(self.p.mover))(body)

    def g1(self):
        @self.stays
        def _():
            for i in range(3):
                self.side(i).wait_recv()
            for i in range(5):
                self.msg(i).start()

    def g2(self):
        @self.stays
        def _():
            for i in range(4):
                self.msg(i).wait_recv()
                self.msg((5, 6, 7, 8)[i]).start()

    def g3(self):
        @self.stays
        def _():
            for i in (5, 6):
                self.msg(i).wait_recv()
                self.msg(4 + i).start()

    def finish(self):
        @pl.when(self.p.mover)
        def _():
            for i in (4, 7, 8, 9, 10):
                self.msg(i).wait_recv()
            drain(self.full.at[0, pl.ds(0, 2)], self.back.at[15])

        @self.stays
        def _():
            drain(self.mine, self.back.at[15])
            for _ in range(2):
                drain(self.sends.at[pl.ds(0, 896)], self.back.at[14])

        for ring in self.first + self.second:
            ring.sent()


class Exchange:
    def __init__(self, place, src_of, dst, everything, sems):
        self.p, self.src_of, self.dst, self.all, self.sems = place, src_of, dst, everything, sems

    def msg(self, k):
        p = self.p
        j = (p.me + k) % 8
        return remote(
            self.src_of(j), self.dst, self.sems.at[0], self.sems.at[k], p.team(j % 2, j // 2)
        )

    def start_pair(self, yy):
        for core in range(2):
            k = (2 * yy + core + 8 - self.p.me) % 8
            pl.when(k != 0)(lambda: self.msg(k).start())

    def wait_pair(self, yy):
        for core in range(2):
            k = (self.p.me + 8 - (2 * yy + core)) % 8
            pl.when(k != 0)(lambda: self.msg(k).wait_recv())

    def start(self):
        @pl.loop(1, 8)
        def _(k):
            self.msg(k).start()

    def wait(self):
        @pl.loop(1, 8)
        def _(k):
            self.msg(k).wait_recv()

    def sent(self):
        drain(self.all.at[pl.ds(0, 896)], self.sems.at[0])


SCRATCH = dict(
    tok=((B, D), BF),
    gain1=((1, D), F32),
    gain2=((1, D), F32),
    cosine=((T, B), F32),
    signed=((T, B), F32),
    h1here=((B, D), BF),
    xb=((B, D), BF),
    cotb=((T, D), BF),
    w=((384, D), BF),
    wo=((T, D), BF),
    wg=((2, FF, D), BF),
    wm=((FF, D), BF),
    h1=((T, D), BF),
    h2=((T, D), BF),
    gb=((T, D), BF),
    y1=((B, D), F32),
    xhat2=((B, D), F32),
    inv2=((B, 1), F32),
    gy=((B, D), F32),
    q=((T, B), BF),
    qt=((2, B, T), BF),
    k=((T, B), BF),
    kt=((B, T), BF),
    v=((T, B), BF),
    vt=((2, 80, T), BF),
    pt=((2, T, T), BF),
    linv=((2, 1, T), F32),
    ot=((B, T), F32),
    o=((T, B), BF),
    orow=((B, D), BF),
    dorow=((B, D), BF),
    dob=((T, B), BF),
    dos=((T, B), BF),
    ds=((2, T, T), BF),
    dqt=((B, T), F32),
    dqkvt=((384, T), BF),
    m=((T, FF), BF),
    da=((T, FF), BF),
    db=((T, FF), BF),
    mt=((FR, T), BF),
    dat=((FR, T), BF),
    dbt=((FR, T), BF),
    gm=((4, 4, 64, D), BF),
    gm_big=((2, 8, 2, 64, 512), BF),
    gm_res=((2, 4, 64, 512), BF),
    gm_small=((2, 8, 64, 256), BF),
    gm_mine=((64, D), BF),
    gm_out=((4, 4, 64, D), BF),
    ga=((512, D), BF),
    ga_slots=((16, 256, B), BF),
    ga_mine=((256, B), BF),
    ga_out=((512, D), BF),
    g1t=((8, 1, D), F32),
    g1p=((16, 1, D), F32),
    g2t=((8, 1, D), F32),
    g2p=((16, 1, D), F32),
    lo_here=((B, D), BF),
    lo_out=((B, D), BF),
    tg_here=((B, D), BF),
    tg_out=((B, D), BF),
)
for _name in ("r2", "ro", "r1"):
    SCRATCH.update(
        {
            _name + "_got": ((512, D), BF),
            _name + "_held": ((512, D), BF),
            _name + "_top": ((64, D), BF),
            _name + "_bottom": ((64, D), BF),
            _name + "_left": ((B, D), BF),
            _name + "_right": ((B, D), BF),
        }
    )
SCRATCH["r2_part"] = ((T, D), BF)
SEMS = dict(
    ag_h1=(12,), ag_wo=(19,), ag_cot=(12,), ag_h2=(12,), ag_gb=(12,),
    rs_r2=(11,), rs_ro=(11,), rs_r1=(11,),
    sm=(4, 7), sm_back=(16,), sa=(12,), g1=(4,), g2=(4,),
    sw_h=(4,), sw_x=(3,), sw_cot=(3,), sw_lo=(3,), sw_tg=(3,),
    f_w=(5,), f_wg=(5,), f_wm=(5,), x_o=(8,), x_do=(8,), outs=(4,), loads=(5,),
)


def kernel(
    tok_in, cot, win, wout, wgate, wmix, gain1_in, gain2_in, cosine_in, signed_in,
    lo_ref, tg_ref, ga_ref, gm_ref, gains_ref, *scratch
):
    names = list(SCRATCH) + ["s_" + n for n in SEMS]
    s = dict(zip(names, scratch, strict=True))
    p = Place()

    class R:
        pass

    r = R()
    r.__dict__.update(s)
    tok, gain1, gain2, cosine, signed = r.tok, r.gain1, r.gain2, r.cosine, r.signed
    loads = [
        pltpu.make_async_copy(src, dst, r.s_loads.at[i])
        for i, (src, dst) in enumerate(
            ((tok_in, tok), (gain1_in, gain1), (cosine_in, cosine), (signed_in, signed), (gain2_in, gain2))
        )
    ]
    loads[0].start()
    loads[1].start()
    own = rows(p.me * B, B)
    other = rows((2 * p.y + 1 - p.c) * B, B)
    own_cols = cols(p.me * B, B)

    def gather(buf, name):
        return Gather(p, buf, s["s_ag_" + name])

    def scatter(name):
        part = r.h2 if name == "r1" else r.r2_part
        parts = [s[name + "_" + n] for n in ("got", "held", "top", "bottom", "left", "right")]
        return Scatter(p, part, *parts, s["s_rs_" + name])

    barrier = pltpu.get_barrier_semaphore()

    @pl.loop(1, 8)
    def _(k):
        j = (p.me + k) % 8
        pl.semaphore_signal(barrier, inc=1, device_id=p.team(j % 2, j // 2), device_id_type=MESH)

    @pl.loop(1, 16)
    def _(k):
        dev = p.plane((p.x + k % 4) % 4, (p.z + k // 4) % 4)
        pl.semaphore_signal(barrier, inc=1, device_id=dev, device_id_type=MESH)

    for d in (1, 3):
        dev = p.plane((p.x + d) % 4, p.z, 1 - p.c)
        pl.semaphore_signal(barrier, inc=1, device_id=dev, device_id_type=MESH)

    for load in loads[2:]:
        load.start()
    loads[0].wait()
    loads[1].wait()
    xhat, _ = norm(tok[...].astype(F32))
    h1here = (xhat * gain1[...]).astype(BF)
    r.h1here[...] = h1here
    pl.when(jnp.logical_not(p.mover))(lambda: r.h1.__setitem__((own, slice(None)), h1here))
    r.qt[...] = jnp.zeros_like(r.qt)
    r.vt[:, 64:80, :] = jnp.ones((2, 16, T), BF)
    r.mt[FF:FR, :] = jnp.zeros((FR - FF, T), BF)
    r.dat[FF:FR, :] = jnp.zeros((FR - FF, T), BF)
    r.dbt[FF:FR, :] = jnp.zeros((FR - FF, T), BF)
    whole_wo = WholeWeight(p, wout, r.wo, r.s_ag_wo)
    whole_wo.near().start()
    sw_cot = Swap(p, cot, r.cotb.at[own], r.s_sw_cot, r.cotb.at[other])
    sw_cot.start_near()
    pl.semaphore_wait(barrier, 24)

    def sw_h(i):
        return remote(
            r.h1here.at[rows(i * 64, 64)],
            r.h1.at[rows((2 * p.y + 1 - p.c) * B + i * 64, 64)],
            r.s_sw_h.at[i],
            r.s_sw_h.at[2 + i],
            p.partner(),
        )

    f_w = Fetch(p, win, r.w, lambda role: rows(role * 128, 128 + role * 128), r.s_f_w)
    f_wg = Fetch(p, wgate, r.wg, lambda i: (slice(None), slice(None), cols(i * 512, 512)), r.s_f_wg)
    f_wm = Fetch(p, wmix, r.wm, lambda i: (slice(None), cols(i * 512, 512)), r.s_f_wm)
    sw_x = Swap(p, tok, r.xb, r.s_sw_x)
    ag_h1, ag_h2, ag_gb = gather(r.h1, "h1"), gather(r.h2, "h2"), gather(r.gb, "gb")
    ag_cot = gather(r.cotb, "cot")

    @pl.when(p.mover)
    def _():
        sw_h(0).start()
        sw_h(1).start()

    f_w.start()
    pl.when(jnp.logical_not(p.mover))(lambda: ag_h1.start())
    whole_wo.w0()
    sw_cot.start_far()

    @pl.when(p.mover)
    def _():
        sw_h(0).wait()
        ag_h1.start_top()
        sw_h(1).wait()
        ag_h1.start_bottom()

    ag_h1.second()
    whole_wo.w1()
    sw_x.start()
    f_w.wait()
    for load in loads[2:]:
        load.wait()

    def project(yy):
        at = rows(yy * 256, 256)
        lanes = cols(yy * 256, 256)
        u = nt(r.h1[at, :], r.w[...])
        co, si = cosine[at, :], signed[at, :]
        q = u[:, :128]
        q = (q * co + swap_halves(q) * si) * (0.125 * LOG2E)
        r.q[at, :] = q.astype(BF)
        qt = q.T.astype(BF)
        r.qt[0, 0:64, lanes] = qt[0:64]
        r.qt[1, 64:128, lanes] = qt[64:128]
        k = u[:, 128:256]
        k = k * co + swap_halves(k) * si
        r.k[at, :] = k.astype(BF)
        r.kt[:, lanes] = k.T.astype(BF)
        v = u[:, 256:]
        r.v[at, :] = v.astype(BF)
        vt = v.T.astype(BF)
        r.vt[0, 0:64, lanes] = vt[0:64]
        r.vt[1, 0:64, lanes] = vt[64:128]

    def early(step):
        @pl.when(step == 3)
        def _():
            sw_cot.wait()
            ag_cot.start()
            whole_wo.w2()
            f_wg.start()
            f_wm.start()

    ag_h1.steps(project, early, True)

    x_o = Exchange(
        p, lambda j: r.o.at[rows(j * B, B)], r.orow.at[:, own_cols], r.o, r.s_x_o
    )

    @pl.loop(0, 4)
    def _(step):
        yy = (p.y + pick(step, 2, 1, 3, 0)) % 4
        lanes = cols(yy * 256, 256)

        pl.when(step == 3)(whole_wo.w3)
        scores = [nn(r.k[...], r.qt[h, :, lanes]) for h in range(2)]
        parts = []
        for h in range(2):
            probs = jnp.exp2(scores[h] - jnp.max(scores[h], 0, keepdims=True)).astype(BF)
            r.pt[h, :, lanes] = probs
            acc = nn(r.vt[h], probs)
            inverse = 1.0 / acc[64:65]
            r.linv[h, :, lanes] = inverse
            parts.append(acc[0:64] * inverse)
        ot = jnp.concatenate(parts, 0)
        r.ot[:, lanes] = ot
        r.o[rows(yy * 256, 256), :] = ot.T.astype(BF)
        x_o.start_pair(yy)

    r.orow[:, own_cols] = r.o[own, :]
    ag_cot.first()
    ag_cot.second()
    sw_x.wait()
    whole_wo.w4()
    x_o.wait()

    x = r.xb[...].astype(F32)
    y1 = x + nn(r.orow[...], r.wo[...])
    r.y1[...] = y1
    xhat, inverse = norm(y1)
    r.xhat2[...] = xhat
    r.inv2[...] = inverse
    r.h2[own, :] = (xhat * gain2[...]).astype(BF)
    ag_h2.start()
    x_o.sent()
    ag_cot.third()
    f_wg.wait()
    f_wm.wait()
    ag_cot.rest()

    def mix(yy):
        at = rows(yy * 256, 256)
        lanes = cols(yy * 256, 256)
        h2 = r.h2[at, :]
        a = nt(h2, r.wg[0])
        b = nt(h2, r.wg[1])
        cdf = 0.5 * (1.0 + lax.erf(a * 0.7071067811865476))
        gelu = a * cdf
        slope = cdf + a * (jnp.exp(-0.5 * a * a) * 0.3989422804014327)
        m = gelu * b
        dm = nt(r.cotb[at, :], r.wm[...]).astype(BF).astype(F32)
        da = dm * b * slope
        db = dm * gelu
        r.m[at, :] = m.astype(BF)
        r.da[at, :] = da.astype(BF)
        r.db[at, :] = db.astype(BF)
        r.mt[0:FF, lanes] = m.T.astype(BF)
        r.dat[0:FF, lanes] = da.T.astype(BF)
        r.dbt[0:FF, lanes] = db.T.astype(BF)

    ag_h2.steps(mix)

    def back_mix(yy):
        at = rows(yy * 256, 256)
        return nn(r.da[at, :], r.wg[0]) + nn(r.db[at, :], r.wg[1])

    rs_2 = scatter("r2")
    rs_2.phase(back_mix)
    sums_m = PlaneSum(
        p, r.gm, r.gm_big, r.gm_res, r.gm_small, r.gm_mine, r.gm_out, r.s_sm, r.s_sm_back, r.r2_part
    )

    def mix_grads(i):
        lanes = cols(i * 256, 256)
        grads = [
            nn(r.mt[...], r.cotb[:, lanes]).astype(BF),
            nn(r.dat[...], r.h2[:, lanes]).astype(BF),
            nn(r.dbt[...], r.h2[:, lanes]).astype(BF),
            jnp.zeros((1024 - 3 * FR, 256), BF),
        ]
        r.gm[:, :, :, lanes] = jnp.concatenate(grads, 0).reshape(4, 4, 64, 256)

    pl.loop(0, 2)(mix_grads)
    sums_m.first[0].s0()
    rs_2.step1()
    pl.loop(2, 4)(mix_grads)
    sums_m.first[1].s0()
    dh2 = rs_2.step2()
    sums_m.first[0].s1()
    sums_m.first[1].s1()

    dx, dgain2 = norm_back(dh2, r.xhat2[...], r.inv2[...], gain2[...])
    gy = r.cotb[own, :].astype(F32) + dx
    r.gy[...] = gy
    r.gb[own, :] = gy.astype(BF)
    r.dorow[...] = nt(r.gb[own, :], r.wo[...]).astype(BF)
    x_do = Exchange(
        p, lambda j: r.dorow.at[:, cols(j * B, B)], r.dob.at[own], r.dob, r.s_x_do
    )
    x_do.start()
    r.dob[own, :] = r.dorow[:, own_cols]
    ag_gb.start()
    gain_2 = Gain(p, r.g2t, r.g2p, r.s_g2)
    gain_2.start(dgain2)
    rs_o = scatter("ro")
    rs_o.phase(lambda yy: nn(r.m[rows(yy * 256, 256), :], r.wm[...]), False)

    @pl.loop(0, 4)
    def _(step):
        yy = (p.y + pick(step, 0, 3, 1, 2)) % 4
        at = rows(yy * 256, 256)
        lanes = cols(yy * 256, 256)

        pl.when(step == 1)(sums_m.to_second)

        @pl.when(step == 3)
        def _():
            sums_m.second[0].s1()
            sums_m.second[1].s1()

        x_do.wait_pair(yy)
        dot = r.dob[at, :].astype(F32).T
        zero = jnp.zeros((64, 256), BF)
        scaled = []
        for h in range(2):
            half = dot[h * 64 : h * 64 + 64] * r.linv[h, :, lanes]
            scaled.append(half)
        dpt = [
            nn(r.v[...], jnp.concatenate([scaled[0].astype(BF), zero], 0)),
            nn(r.v[...], jnp.concatenate([zero, scaled[1].astype(BF)], 0)),
        ]
        r.dos[at, :] = jnp.concatenate(scaled, 0).T.astype(BF)
        for h in range(2):
            half = slice(h * 64, h * 64 + 64)
            weighted = jnp.sum(scaled[h] * r.ot[half, lanes], 0, keepdims=True)
            ds = (r.pt[h, :, lanes].astype(F32) * (dpt[h] - weighted)).astype(BF)
            r.ds[h, :, lanes] = ds
            r.dqt[half, lanes] = nn(r.kt[half, :], ds)

    x_do.sent()

    def back_project(yy):
        at = rows(yy * 256, 256)
        lanes = cols(yy * 256, 256)
        first = lax.broadcasted_iota(jnp.int32, (256, B), 1) < 64
        dk = jnp.where(first, nn(r.ds[0, at, :], r.q[...]), nn(r.ds[1, at, :], r.q[...])) * (1 / LOG2E)
        dv = jnp.where(first, nn(r.pt[0, at, :], r.dos[...]), nn(r.pt[1, at, :], r.dos[...]))
        co, si = cosine[at, :], signed[at, :]
        dq = r.dqt[:, lanes].T * 0.125
        dq = dq * co - swap_halves(dq) * si
        dk = dk * co - swap_halves(dk) * si
        r.dqkvt[0:128, lanes] = dq.T.astype(BF)
        r.dqkvt[128:256, lanes] = dk.T.astype(BF)
        r.dqkvt[256:384, lanes] = dv.T.astype(BF)
        dqkv = jnp.concatenate([dq.astype(BF), dk.astype(BF), dv.astype(BF)], 1)
        return nn(dqkv, r.w[...])

    rs_1 = scatter("r1")

    def late(step):
        @pl.when(step == 0)
        def _():
            ag_gb.first()
            ag_gb.second()

        @pl.when(step == 1)
        def _():
            sums_m.to_mine()
            sums_m.g0()

    rs_1.phase(back_project, True, late)
    rs_1.step1()
    sums_m.g1()
    sums_a = Sums(
        p, r.ga, r.ga_slots, r.ga_mine, r.ga_out, r.s_sa
    )
    ag_gb.third()
    ag_gb.rest()

    @pl.loop(0, 4)
    def _(i):
        off = (i + 2) % 4
        lanes = cols(((p.z + off) % 4) * 256, 256)
        r.ga[0:384, lanes] = nn(r.dqkvt[...], r.h1[:, lanes]).astype(BF)
        r.ga[384:512, lanes] = nn(r.ot[...].astype(BF), r.gb[:, lanes]).astype(BF)
        sums_a.spread(off)

    rs_o.step0()
    rs_o.step_right()
    rs_o.step_left()
    dh1 = rs_1.step2()
    xhat, inverse = norm(r.xb[...].astype(F32))
    dx, dgain1 = norm_back(dh1, xhat, inverse, gain1[...])
    gain_1 = Gain(p, r.g1t, r.g1p, r.s_g1)
    gain_1.start(dgain1)
    r.tg_here[...] = (r.gy[...] + dx).astype(BF)
    sw_tg = Swap(p, r.tg_here, r.tg_out, r.s_sw_tg)
    sw_tg.start()
    sums_m.g2()
    rs_o.step1()
    sums_a.add()
    sums_a.give()
    gain_2.middle()
    gain_1.middle()
    r.lo_here[...] = (r.y1[...] + rs_o.step2()).astype(BF)
    sw_lo = Swap(p, r.lo_here, r.lo_out, r.s_sw_lo)
    sw_lo.start()
    sw_tg.wait()
    tg_copy = pltpu.make_async_copy(r.tg_out, tg_ref, r.s_outs.at[0])
    tg_copy.start()
    sums_m.g3()
    sums_a.take()
    sums_m.finish()
    gm_copy = pltpu.make_async_copy(r.gm_out, gm_ref, r.s_outs.at[1])
    gm_copy.start()
    gains_ref[1:2, :] = gain_2.end()
    gains_ref[0:1, :] = gain_1.end()
    sw_lo.wait()
    lo_copy = pltpu.make_async_copy(r.lo_out, lo_ref, r.s_outs.at[2])
    lo_copy.start()
    sums_a.finish()
    ga_copy = pltpu.make_async_copy(r.ga_out, ga_ref, r.s_outs.at[3])
    ga_copy.start()
    for copy in [lo_copy, tg_copy, gm_copy, ga_copy]:
        copy.wait()


def widen(
    lo, tg, ga, gm, gains, lo_ref, tg_ref, gi_ref, go_ref, gg_ref, gm_ref, first_ref, second_ref,
    lo_in, tg_in, ga_in, gm_in, tg_out, ga_out, gm_out, sems,
):
    pieces = [(gm, gm_in, gm_out, i * FR, FF, target) for i, target in enumerate((gm_ref, gg_ref.at[0], gg_ref.at[1]))]
    pieces += [(ga, ga_in, ga_out, 0, 384, gi_ref), (ga, ga_in, ga_out, 384, B, go_ref)]
    pieces += [(tg, tg_in, tg_out, 0, B, tg_ref)]
    loads, stores = [], []
    for i, (src, held, _, first, size, _) in enumerate(pieces):
        part = pl.ds(first, FR if size == FF else size)
        loads.append(pltpu.make_async_copy(src.at[part], held.at[part], sems.at[i]))
    loads.append(pltpu.make_async_copy(lo, lo_in, sems.at[6]))
    for load in loads:
        load.start()
    for i in range(8):
        first_ref[i : i + 1, :] = gains[0:1, i * B : i * B + B]
        second_ref[i : i + 1, :] = gains[1:2, i * B : i * B + B]
    for i, (_, held, wide, first, size, target) in enumerate(pieces):
        loads[i].wait()
        wide[first : first + size, :] = held[first : first + size, :].astype(F32)
        stores.append(pltpu.make_async_copy(wide.at[pl.ds(first, size)], target, sems.at[7 + i]))
        stores[-1].start()
    loads[6].wait()
    stores.append(pltpu.make_async_copy(lo_in, lo_ref, sems.at[13]))
    stores[-1].start()
    for store in stores:
        store.wait()


def local(tokens, attn_in, attn_out, mlp_in, mlp_out, norm_first, norm_second, cotangent):
    cosine, signed = tables()
    any_space = pl.BlockSpec(memory_space=pl.ANY)
    vmem = pl.BlockSpec(memory_space=pltpu.VMEM)
    limit = 63 * 1024 * 1024
    shapes = [(B, D), (B, D), (512, D), (4, 4, 64, D)]
    lo, tg, ga, gm, gains = pl.pallas_call(
        kernel,
        out_shape=tuple(jax.ShapeDtypeStruct(shape, BF) for shape in shapes)
        + (jax.ShapeDtypeStruct((2, D), F32),),
        in_specs=[any_space] * 10,
        out_specs=(any_space,) * 4 + (vmem,),
        scratch_shapes=[pltpu.VMEM(shape, kind) for shape, kind in SCRATCH.values()]
        + [pltpu.SemaphoreType.DMA(shape) for shape in SEMS.values()],
        compiler_params=pltpu.CompilerParams(
            collective_id=0, has_side_effects=True, vmem_limit_bytes=limit
        ),
    )(
        tokens,
        cotangent,
        attn_in.transpose(1, 2, 3, 0).reshape(384, D),
        attn_out.reshape(B, D),
        mlp_in.transpose(0, 2, 1),
        mlp_out,
        norm_first.reshape(1, D),
        norm_second.reshape(1, D),
        jnp.asarray(cosine),
        jnp.asarray(signed),
    )
    wide = [(B, D), (384, D), (B, D), (2, FF, D), (FF, D), (8, B), (8, B)]
    lo, tg, gi, go, gg, gm, first, second = pl.pallas_call(
        widen,
        out_shape=(jax.ShapeDtypeStruct((B, D), BF),)
        + tuple(jax.ShapeDtypeStruct(shape, F32) for shape in wide),
        in_specs=[any_space] * 4 + [vmem],
        out_specs=(any_space,) * 6 + (vmem, vmem),
        scratch_shapes=[
            pltpu.VMEM((B, D), BF),
            pltpu.VMEM((B, D), BF),
            pltpu.VMEM((512, D), BF),
            pltpu.VMEM((1024, D), BF),
            pltpu.VMEM((B, D), F32),
            pltpu.VMEM((512, D), F32),
            pltpu.VMEM((3 * FR, D), F32),
            pltpu.SemaphoreType.DMA((14,)),
        ],
        compiler_params=pltpu.CompilerParams(vmem_limit_bytes=limit),
    )(lo, tg, ga, gm.reshape(1024, D), gains)
    return (
        lo,
        tg,
        gi.reshape(3, 2, 64, D).transpose(3, 0, 1, 2),
        go.reshape(2, 64, D),
        gg.transpose(0, 2, 1),
        gm,
        first.reshape(D),
        second.reshape(D),
    )


def solution(mesh):
    placed = (
        P(("dp", "tensor"), None),
        P(None, None, "tensor", None),
        P("tensor", None, None),
        P(None, None, "tensor"),
        P("tensor", None),
        P(),
        P(),
        P(("dp", "tensor"), None),
    )
    return jax.shard_map(
        local,
        mesh=mesh,
        in_specs=placed,
        out_specs=(
            P(("dp", "tensor"), None),
            P(("dp", "tensor"), None),
            P(None, None, "tensor", None),
            P("tensor", None, None),
            P(None, None, "tensor"),
            P("tensor", None),
            P(),
            P(),
        ),
        check_vma=False,
    )
```

```python
import jax
import jax.numpy as jnp
import numpy as np
from jax import lax
from jax.experimental import pallas as pl
from jax.experimental.pallas import tpu as pltpu
from jax.sharding import PartitionSpec as P

MESH = pl.DeviceIdType.MESH
BF = jnp.bfloat16
F32 = jnp.float32
EPS = 1e-05
THETA = 160000.0
T = 1024
D = 1024
B = 128
FF = 328
FR = 336
LOG2E = 1.4426950408889634


def tables():
    places = np.arange(T, dtype=np.float32)
    frequency = (THETA ** (-np.arange(0, 64, 2, dtype=np.float32) / 64)).astype(np.float32)
    angles = places[:, None] * frequency[None, :]
    cosine, sine = np.cos(angles), np.sin(angles)
    cosine = np.concatenate([cosine, cosine] * 2, -1)
    signed = np.concatenate([-sine, sine] * 2, -1)
    order = np.concatenate([np.arange(B) + ((j % 2) * 4 + j // 2) * B for j in range(8)])
    return cosine[order].astype(np.float32), signed[order].astype(np.float32)


def nn(a, b):
    return jnp.dot(a, b, preferred_element_type=F32)


def nt(a, b):
    return lax.dot_general(a, b, (((1,), (1,)), ((), ())), preferred_element_type=F32)


def pick(step, a, b, c, d):
    return jnp.where(step == 0, a, jnp.where(step == 1, b, jnp.where(step == 2, c, d)))


def swap_halves(u):
    lane = lax.broadcasted_iota(jnp.int32, u.shape, 1)
    return jnp.where((lane % 64) < 32, pltpu.roll(u, 96, 1), pltpu.roll(u, 32, 1))


def norm(v):
    centred = v - jnp.mean(v, -1, keepdims=True)
    inverse = lax.rsqrt(jnp.mean(centred * centred, -1, keepdims=True) + EPS)
    return centred * inverse, inverse


def norm_back(gradient, xhat, inverse, gain):
    e = gradient * gain
    dx = inverse * (
        e - jnp.mean(e, -1, keepdims=True) - xhat * jnp.mean(e * xhat, -1, keepdims=True)
    )
    return dx, jnp.sum(gradient * xhat, 0, keepdims=True)


def rows(start, size):
    return pl.ds(pl.multiple_of(start, 16), size)


def cols(start, size):
    return pl.ds(pl.multiple_of(start, 128), size)


def remote(src, dst, ssem, rsem, dev):
    return pltpu.make_async_remote_copy(
        src_ref=src, dst_ref=dst, send_sem=ssem, recv_sem=rsem, device_id=dev, device_id_type=MESH
    )


def drain(ref, sem):
    pltpu.make_async_copy(ref, ref, sem).wait()


class Place:
    def __init__(self):
        dp, tensor = lax.axis_index("dp"), lax.axis_index("tensor")
        self.dp, self.tensor = dp, tensor
        self.c = dp % 2
        self.xlo, self.y = tensor // 4, tensor % 4
        self.z = dp // 4
        self.x = ((dp // 2) % 2) * 2 + self.xlo
        self.me = 2 * self.y + self.c
        self.mover = self.c != self.xlo
        self.right, self.left = (self.y + 1) % 4, (self.y + 3) % 4
        self.opp = (self.y + 2) % 4

    def team(self, core, y):
        return {"dp": self.dp - self.c + core, "tensor": self.xlo * 4 + y}

    def plane(self, x, z, core=None):
        core = self.c if core is None else core
        return {"dp": z * 4 + (x // 2) * 2 + core, "tensor": (x % 2) * 4 + self.y}

    def partner(self):
        return {"dp": self.dp - self.c + self.xlo, "tensor": self.c * 4 + self.y}


class Gather:
    def __init__(self, place, buf, sems):
        self.p, self.buf, self.sems = place, buf, sems

    def msg(self, i):
        p = self.p
        me, lt, rt, op = p.me, 2 * p.left + p.c, 2 * p.right + p.c, 2 * p.opp + p.c
        right, left = p.team(p.c, p.right), p.team(p.c, p.left)
        sib = p.team(1 - p.c, p.y)
        block, first, size, dev = (
            (me, 0, 64, right),
            (me, 64, 64, left),
            (me, 64, 64, right),
            (me, 0, 64, left),
            (me, 0, 128, sib),
            (lt, 0, 64, right),
            (rt, 64, 64, left),
            (lt, 0, 128, sib),
            (rt, 0, 128, sib),
            (op, 0, 64, sib),
            (op, 64, 64, sib),
        )[i]
        ref = self.buf.at[rows(block * B + first, size)]
        return remote(ref, ref, self.sems.at[11], self.sems.at[i], dev)

    def start(self):
        for i in range(5):
            self.msg(i).start()

    def start_top(self):
        self.msg(0).start()
        self.msg(3).start()

    def start_bottom(self):
        self.msg(1).start()
        self.msg(2).start()
        self.msg(4).start()

    def first(self):
        self.msg(4).wait_recv()

    def second(self):
        self.msg(0).wait_recv()
        self.msg(5).start()
        self.msg(1).wait_recv()
        self.msg(6).start()
        self.msg(2).wait_recv()
        self.msg(7).start()
        self.msg(3).wait_recv()
        self.msg(8).start()

    def third(self):
        self.msg(5).wait_recv()
        self.msg(9).start()
        self.msg(6).wait_recv()
        self.msg(10).start()

    def left_in(self):
        self.msg(7).wait_recv()

    def right_in(self):
        self.msg(8).wait_recv()

    def opp_in(self):
        self.msg(9).wait_recv()
        self.msg(10).wait_recv()

    def sent(self):
        drain(self.buf.at[pl.ds(0, 896)], self.sems.at[11])

    def rest(self):
        self.left_in()
        self.right_in()
        self.opp_in()
        self.sent()

    def steps(self, body, hook=None, forwarded=False, idle=None):
        p = self.p

        @pl.loop(0, 4)
        def _(step):
            @pl.when(step == 0)
            def _():
                self.first()

            @pl.when(step == 1)
            def _():
                if idle is not None:
                    idle()
                if not forwarded:
                    self.second()
                self.left_in()

            @pl.when(step == 2)
            def _():
                self.right_in()

            @pl.when(step == 3)
            def _():
                self.third()
                self.opp_in()

            if hook is not None:
                hook(step)
            body((p.y + pick(step, 0, 3, 1, 2)) % 4)

        self.sent()


class Scatter:
    def __init__(self, place, part, got, held, top, bottom, from_left, from_right, sems):
        self.p = place
        self.part, self.got, self.held = part, got, held
        self.top, self.bottom = top, bottom
        self.from_left, self.from_right = from_left, from_right
        self.sems = sems

    def off(self, step):
        return pick(step, 2, 1, 3, 0)

    def sib(self, step):
        p = self.p
        yy = (p.y + self.off(step)) % 4
        return remote(
            self.part.at[rows((2 * yy + 1 - p.c) * B, B)],
            self.got.at[rows(yy * B, B)],
            self.sems.at[10],
            self.sems.at[step],
            p.team(1 - p.c, p.y),
        )

    def msg(self, i):
        p = self.p
        right, left = p.team(p.c, p.right), p.team(p.c, p.left)
        block, first, dst, dev = (
            (p.opp, 0, self.top, right),
            (p.opp, 64, self.bottom, left),
            (p.right, 64, self.from_left.at[rows(64, 64)], right),
            (p.right, 0, self.from_left.at[rows(0, 64)], right),
            (p.left, 0, self.from_right.at[rows(0, 64)], left),
            (p.left, 64, self.from_right.at[rows(64, 64)], left),
        )[i]
        return remote(
            self.held.at[rows(block * B + first, 64)], dst, self.sems.at[10], self.sems.at[4 + i], dev
        )

    def phase(self, compute, early=True, hook=None):
        p = self.p

        @pl.loop(0, 4)
        def _(step):
            yy = (p.y + self.off(step)) % 4
            self.part[rows(yy * 256, 256), :] = compute(yy).astype(BF)
            self.sib(step).start()
            if early:
                pl.when(step == 1)(self.step0)
                pl.when(step == 2)(self.step_right)
                pl.when(step == 3)(self.step_left)
            if hook is not None:
                hook(step)

    def pair_sum(self, yy):
        own = self.part[rows((2 * yy + self.p.c) * B, B), :].astype(F32)
        return own + self.got[rows(yy * B, B), :].astype(F32)

    def step0(self):
        p = self.p
        self.sib(0).wait_recv()
        self.held[rows(p.opp * B, B), :] = self.pair_sum(p.opp).astype(BF)
        self.msg(0).start()
        self.msg(1).start()

    def step_right(self):
        p = self.p
        self.sib(1).wait_recv()
        self.held[rows(p.right * B, B), :] = self.pair_sum(p.right).astype(BF)
        self.msg(2).start()

    def step_left(self):
        p = self.p
        self.sib(2).wait_recv()
        self.held[rows(p.left * B, B), :] = self.pair_sum(p.left).astype(BF)
        self.msg(4).start()

    def step1(self):
        p = self.p
        top, bottom = rows(p.right * B, 64), rows(p.left * B + 64, 64)
        self.msg(0).wait_recv()
        self.held[top, :] = (self.held[top, :].astype(F32) + self.top[...].astype(F32)).astype(BF)
        self.msg(3).start()
        self.msg(1).wait_recv()
        self.held[bottom, :] = (
            self.held[bottom, :].astype(F32) + self.bottom[...].astype(F32)
        ).astype(BF)
        self.msg(5).start()

    def step2(self):
        p = self.p
        self.sib(3).wait_recv()
        total = self.pair_sum(p.y)
        for i in range(2, 6):
            self.msg(i).wait_recv()
        total = total + self.from_left[...].astype(F32) + self.from_right[...].astype(F32)
        drain(self.part.at[pl.ds(0, 896)], self.sems.at[10])
        return total


class Gain:
    def __init__(self, place, team_buf, plane_buf, sems):
        self.p, self.team_buf, self.plane_buf, self.sems = place, team_buf, plane_buf, sems

    def start(self, value):
        p = self.p
        ref = self.team_buf.at[p.me]
        ref[...] = value

        @pl.loop(1, 8)
        def _(k):
            j = (p.me + k) % 8
            remote(ref, ref, self.sems.at[0], self.sems.at[1], p.team(j % 2, j // 2)).start()

    def middle(self):
        p = self.p
        drain(self.team_buf.at[pl.ds(0, 7)], self.sems.at[1])
        ref = self.plane_buf.at[p.z * 4 + p.x]
        ref[...] = jnp.sum(self.team_buf[...], 0)

        @pl.loop(1, 16)
        def _(k):
            dev = p.plane((p.x + k % 4) % 4, (p.z + k // 4) % 4)
            remote(ref, ref, self.sems.at[2], self.sems.at[3], dev).start()

        drain(self.team_buf.at[pl.ds(0, 7)], self.sems.at[0])

    def end(self):
        drain(self.plane_buf.at[pl.ds(0, 15)], self.sems.at[3])
        total = jnp.sum(self.plane_buf[...], 0)
        drain(self.plane_buf.at[pl.ds(0, 15)], self.sems.at[2])
        return total


class Swap:
    def __init__(self, place, src, dst, sems, there=None):
        self.p, self.src, self.dst, self.sems = place, src, dst, sems
        self.there = dst if there is None else there

    def far(self):
        return remote(self.src, self.there, self.sems.at[0], self.sems.at[1], self.p.partner())

    def near(self):
        return pltpu.make_async_copy(self.src, self.dst, self.sems.at[2])

    def start(self):
        self.start_far()
        self.start_near()

    def start_far(self):
        pl.when(self.p.mover)(lambda: self.far().start())

    def start_near(self):
        pl.when(jnp.logical_not(self.p.mover))(lambda: self.near().start())

    def wait(self):
        pl.when(self.p.mover)(lambda: self.far().wait())
        pl.when(jnp.logical_not(self.p.mover))(lambda: self.near().wait())


class Fetch:
    def __init__(self, place, src, dst, part, sems):
        self.p, self.src, self.dst, self.part, self.sems = place, src, dst, part, sems

    def far(self, role):
        p = self.p
        step = 1 + 2 * ((p.x + role) % 2)
        part = self.part(role)
        return remote(
            self.src.at[part],
            self.dst.at[part],
            self.sems.at[role],
            self.sems.at[2 + role],
            p.plane((p.x + step) % 4, p.z, p.xlo),
        )

    def near(self):
        return pltpu.make_async_copy(self.src, self.dst, self.sems.at[4])

    def start(self):
        self.start_away()
        self.start_partner()

    def start_away(self):
        pl.when(self.p.mover)(lambda: self.far(1).start())
        pl.when(jnp.logical_not(self.p.mover))(lambda: self.near().start())

    def start_partner(self):
        pl.when(self.p.mover)(lambda: self.far(0).start())

    def wait(self):
        @pl.when(self.p.mover)
        def _():
            self.far(0).wait()
            self.far(1).wait()

        pl.when(jnp.logical_not(self.p.mover))(lambda: self.near().wait())


class WholeWeight:
    def __init__(self, place, src, buf, sems):
        self.p, self.src, self.buf, self.sems = place, src, buf, sems

    def near(self):
        p = self.p
        return pltpu.make_async_copy(
            self.src, self.buf.at[rows((2 * p.y + p.xlo) * B, B)], self.sems.at[18]
        )

    def msg(self, i):
        p = self.p
        right, left = p.team(p.c, p.right), p.team(p.c, p.left)
        sib = p.team(1 - p.c, p.y)
        side = p.plane((p.x + 1 + 2 * p.c) % 4, p.z)
        ys = (p.y, p.left, p.right, p.opp)
        first, size = 0, 64
        if i < 6:
            y, first, size, dev = (
                (p.y, 0, 32, right),
                (p.y, 32, 32, left),
                (p.y, 32, 32, right),
                (p.y, 0, 32, left),
                (p.left, 0, 32, right),
                (p.right, 32, 32, left),
            )[i]
            group = p.xlo
        elif i < 10:
            y, group, dev = ys[i - 6], p.xlo, side
        elif i < 13:
            y, group, dev = ys[i - 9], p.xlo, sib
        else:
            y, group, dev = ys[i - 13], 1 - p.xlo, sib
        ref = self.buf.at[rows((2 * y + group) * B + p.c * 64 + first, size)]
        return remote(ref, ref, self.sems.at[17], self.sems.at[i], dev)

    def go(self, *which):
        for i in which:
            self.msg(i).start()

    def got(self, *which):
        for i in which:
            self.msg(i).wait_recv()

    def w0(self):
        self.near().wait()
        self.go(0, 1, 2, 3)

    def w1(self):
        self.go(6)
        self.got(0)
        self.go(4)
        self.got(1)
        self.go(5)
        self.got(2)
        self.go(7, 10)
        self.got(3)
        self.go(8, 11)

    def w2(self):
        self.got(4, 5)
        self.go(9, 12)

    def w3(self):
        for i in range(4):
            self.got(6 + i)
            self.go(13 + i)

    def w4(self):
        self.got(*range(10, 17))
        drain(self.buf.at[pl.ds(0, 896)], self.sems.at[17])


class AxisSum:
    def __init__(self, i, dev, blk, bufs, sems):
        self.i, self.dev, self.blk, self.bufs, self.sems = i, dev, blk, bufs, sems

    def start(self):
        for k in (2, 1, 3):
            j = (self.i + k) % 4
            remote(
                self.blk(j), self.bufs.at[k - 1], self.sems.at[1], self.sems.at[0], self.dev(j)
            ).start()

    def total(self):
        drain(self.bufs, self.sems.at[0])
        total = self.blk(self.i)[...].astype(F32)
        for k in range(3):
            total = total + self.bufs[k].astype(F32)
        return total.astype(BF)

    def sent(self):
        drain(self.bufs, self.sems.at[1])


class PlaneSum:
    def __init__(self, place, full, big, res, small, mine, out, sems, back):
        p = self.p = place
        self.full, self.mine, self.out, self.back, self.res = full, mine, out, back, res
        along_z = p.z, lambda j: p.plane(p.x, j)
        along_x = p.x, lambda j: p.plane(j, p.z)
        self.half = half = full.shape[3] // 2
        self.first = (
            AxisSum(*along_z, lambda j: full.at[j, :, :, pl.ds(0, half)], big.at[0], sems.at[0]),
            AxisSum(*along_x, lambda j: full.at[:, j, :, pl.ds(half, half)], big.at[1], sems.at[1]),
        )
        self.second = (
            AxisSum(*along_x, lambda j: res.at[0, j], small.at[0], sems.at[2]),
            AxisSum(*along_z, lambda j: res.at[1, j], small.at[1], sems.at[3]),
        )

    def to_second(self, *which):
        for n in which:
            self.res[n] = self.first[n].total()
            self.second[n].start()

    def to_mine(self):
        for n in range(2):
            self.mine[:, n * self.half : (n + 1) * self.half] = self.second[n].total()

    def give_msg(self, k):
        p = self.p
        dev = p.plane((p.x + k % 4) % 4, (p.z + k // 4) % 4)
        ref = self.out.at[p.z, p.x]
        return remote(self.mine, ref, self.back.at[0], self.back.at[2 + k // 4], dev)

    def give(self):
        p = self.p

        @pl.loop(0, 8)
        def _(i):
            k = (i // 2) * 4 + (i % 2) * 2 + jnp.where(p.mover, 1, 0)
            pl.when(k != 0)(lambda: self.give_msg(k).start())

        @self.stays
        def _():
            self.out[p.z, p.x] = self.mine[...]

    def forward(self, i):
        p = self.p
        block = self.out.at[(p.z + 4 - i) % 4]
        return remote(block, block, self.back.at[1], self.back.at[6 + i], p.team(1 - p.c, p.y))

    def to(self, i, target, sem):
        block = (self.p.z + 4 - i) % 4
        return pltpu.make_async_copy(self.out.at[block], target.at[block], sem)

    def take(self, target, sem):
        @self.stays
        def _():
            for i in range(4):
                drain(self.out.at[0, pl.ds(0, 4 if i else 3)], self.back.at[2 + i])
                self.forward(i).start()
                self.to(i, target, sem).start()

        @pl.when(self.p.mover)
        def _():
            for i in range(4):
                self.forward(i).wait_recv()
                self.to(i, target, sem).start()

    def taken(self):
        @pl.when(self.p.mover)
        def _():
            drain(self.out.at[pl.ds(0, 2)], self.back.at[0])

        @self.stays
        def _():
            drain(self.out, self.back.at[1])
            drain(self.full.at[0], self.back.at[0])
            drain(self.full.at[1, pl.ds(0, 3)], self.back.at[0])

        for axis in self.first + self.second:
            axis.sent()

    def stays(self, body):
        pl.when(jnp.logical_not(self.p.mover))(body)


class StagedPlaneSum(PlaneSum):
    def side(self, i):
        p = self.p
        return remote(
            self.mine,
            self.out.at[p.z, p.x],
            self.back.at[15],
            self.back.at[11 + i],
            p.plane((p.x + (1, 3, 2)[i]) % 4, p.z),
        )

    def msg(self, i):
        p = self.p
        lt, rt, op = (p.z + 3) % 4, (p.z + 1) % 4, (p.z + 2) % 4
        right, left, sib = p.plane(p.x, rt), p.plane(p.x, lt), p.team(1 - p.c, p.y)
        block, first, size, dev = (
            (p.z, 0, 2, right),
            (p.z, 2, 2, left),
            (p.z, 2, 2, right),
            (p.z, 0, 2, left),
            (p.z, 0, 4, sib),
            (lt, 0, 2, right),
            (rt, 2, 2, left),
            (lt, 0, 4, sib),
            (rt, 0, 4, sib),
            (op, 0, 2, sib),
            (op, 2, 2, sib),
        )[i]
        ref = self.out.at[block, pl.ds(first, size)]
        return remote(ref, ref, self.back.at[14], self.back.at[i], dev)

    def g0(self):
        p = self.p

        @pl.when(p.mover)
        def _():
            self.side(0).start()
            self.side(1).start()

        @pl.when(jnp.logical_not(p.mover))
        def _():
            self.side(2).start()
            self.out[p.z, p.x] = self.mine[...]

    def g1(self):
        @self.stays
        def _():
            for i in range(3):
                self.side(i).wait_recv()
            for i in range(5):
                self.msg(i).start()

    def g2(self):
        @self.stays
        def _():
            for i in range(4):
                self.msg(i).wait_recv()
                self.msg((5, 6, 7, 8)[i]).start()

    def g3(self):
        @self.stays
        def _():
            for i in (5, 6):
                self.msg(i).wait_recv()
                self.msg(4 + i).start()

    def finish(self):
        @pl.when(self.p.mover)
        def _():
            for i in (4, 7, 8, 9, 10):
                self.msg(i).wait_recv()
            drain(self.full.at[0, pl.ds(0, 2)], self.back.at[15])

        @self.stays
        def _():
            drain(self.mine, self.back.at[15])
            drain(self.out, self.back.at[14])
            drain(self.out.at[pl.ds(0, 3)], self.back.at[14])

        for axis in self.first + self.second:
            axis.sent()


class Exchange:
    def __init__(self, place, src_of, dst, everything, sems):
        self.p, self.src_of, self.dst, self.all, self.sems = place, src_of, dst, everything, sems

    def msg(self, k):
        p = self.p
        j = (p.me + k) % 8
        return remote(
            self.src_of(j), self.dst, self.sems.at[0], self.sems.at[k], p.team(j % 2, j // 2)
        )

    def start_pair(self, yy):
        for core in range(2):
            k = (2 * yy + core + 8 - self.p.me) % 8
            pl.when(k != 0)(lambda: self.msg(k).start())

    def wait(self):
        @pl.loop(1, 8)
        def _(k):
            self.msg(k).wait_recv()

    def wait_pair(self, yy):
        for core in range(2):
            k = (self.p.me + 8 - (2 * yy + core)) % 8
            pl.when(k != 0)(lambda: self.msg(k).wait_recv())

    def start(self):
        @pl.loop(1, 8)
        def _(k):
            self.msg(k).start()

    def sent(self):
        drain(self.all.at[pl.ds(0, 896)], self.sems.at[0])


SCRATCH = dict(
    tok=((B, D), BF),
    gain1=((1, D), F32),
    gain2=((1, D), F32),
    cosine=((T, B), F32),
    signed=((T, B), F32),
    xb=((B, D), BF),
    cotb=((T, D), BF),
    w=((384, D), BF),
    wo=((T, D), BF),
    wg=((2, FF, D), BF),
    wm=((FF, D), BF),
    h1=((T, D), BF),
    h2=((T, D), BF),
    gb=((T, D), BF),
    y1=((B, D), F32),
    xhat2=((B, D), F32),
    inv2=((B, 1), F32),
    gy=((B, D), F32),
    q=((T, B), BF),
    dqkv=((T, 384), BF),
    qt=((2, B, T), BF),
    k=((T, B), BF),
    kt=((B, T), BF),
    v=((T, B), BF),
    vt=((2, 80, T), BF),
    pt=((2, T, T), BF),
    linv=((2, 1, T), F32),
    ot=((B, T), F32),
    o=((T, B), BF),
    orow=((B, D), BF),
    dos=((T, B), BF),
    ds=((2, T, T), BF),
    dqt=((B, T), F32),
    dqkvt=((384, T), BF),
    m=((T, FF), BF),
    da=((T, FF), BF),
    db=((T, FF), BF),
    mt=((FR, T), BF),
    dat=((FR, T), BF),
    dbt=((FR, T), BF),
    gm=((4, 4, 64, D), BF),
    gm_big=((2, 3, 4, 64, 512), BF),
    gm_res=((2, 4, 64, 512), BF),
    gm_small=((2, 3, 64, 512), BF),
    gm_mine=((64, D), BF),
    gm_out=((4, 4, 64, D), BF),
    ga=((4, 4, 48, 512), BF),
    ga_big=((2, 3, 4, 48, 256), BF),
    ga_res=((2, 4, 48, 256), BF),
    ga_small=((2, 3, 48, 256), BF),
    ga_mine=((48, 512), BF),
    ga_out=((4, 4, 48, 512), BF),
    go=((4, 4, 16, 512), BF),
    go_big=((2, 3, 4, 16, 256), BF),
    go_res=((2, 4, 16, 256), BF),
    go_small=((2, 3, 16, 256), BF),
    go_mine=((16, 512), BF),
    go_out=((4, 4, 16, 512), BF),
    dorow=((B, D), BF),
    dob=((T, B), BF),
    g1t=((8, 1, D), F32),
    g1p=((16, 1, D), F32),
    g2t=((8, 1, D), F32),
    g2p=((16, 1, D), F32),
    lo_here=((B, D), BF),
    lo_out=((B, D), BF),
    tg_here=((B, D), BF),
    tg_out=((B, D), BF),
)
for _name in ("r2", "ro", "r1"):
    SCRATCH.update(
        {
            _name + "_got": ((512, D), BF),
            _name + "_held": ((512, D), BF),
            _name + "_top": ((64, D), BF),
            _name + "_bottom": ((64, D), BF),
            _name + "_left": ((B, D), BF),
            _name + "_right": ((B, D), BF),
        }
    )
SCRATCH["r2_part"] = ((T, D), BF)
SEMS = dict(
    ag_h1=(12,), ag_wo=(19,), ag_cot=(12,), ag_h2=(12,), ag_gb=(12,),
    rs_r2=(11,), rs_ro=(11,), rs_r1=(11,),
    sm=(4, 2), sm_back=(16,), sa=(4, 2), sa_back=(10,), so=(4, 2), so_back=(10,), g1=(4,), g2=(4,),
    sw_x=(4,), sw_cot=(3,), sw_lo=(3,), sw_tg=(3,),
    f_w=(5,), f_wg=(2, 5), f_wm=(5,), x_o=(8,), x_do=(8,), outs=(5,), loads=(5,),
)


def kernel(
    tok_in, cot, win, wout, wgate, wmix, gain1_in, gain2_in, cosine_in, signed_in,
    lo_ref, tg_ref, ga_ref, go_ref, gm_ref, gains_ref, *scratch
):
    names = list(SCRATCH) + ["s_" + n for n in SEMS]
    s = dict(zip(names, scratch, strict=True))
    p = Place()

    class R:
        pass

    r = R()
    r.__dict__.update(s)
    tok, gain1, gain2, cosine, signed = r.tok, r.gain1, r.gain2, r.cosine, r.signed
    loads = [
        pltpu.make_async_copy(src, dst, r.s_loads.at[i])
        for i, (src, dst) in enumerate(
            ((tok_in, tok), (gain1_in, gain1), (cosine_in, cosine), (signed_in, signed), (gain2_in, gain2))
        )
    ]
    loads[0].start()
    loads[1].start()
    own = rows(p.me * B, B)
    other = rows((2 * p.y + 1 - p.c) * B, B)
    own_cols = cols(p.me * B, B)

    def gather(buf, name):
        return Gather(p, buf, s["s_ag_" + name])

    def scatter(name):
        part = r.h2 if name == "r1" else r.r2_part
        parts = [s[name + "_" + n] for n in ("got", "held", "top", "bottom", "left", "right")]
        return Scatter(p, part, *parts, s["s_rs_" + name])

    barrier = pltpu.get_barrier_semaphore()

    @pl.loop(1, 8)
    def _(k):
        j = (p.me + k) % 8
        pl.semaphore_signal(barrier, inc=1, device_id=p.team(j % 2, j // 2), device_id_type=MESH)

    @pl.loop(1, 16)
    def _(k):
        dev = p.plane((p.x + k % 4) % 4, (p.z + k // 4) % 4)
        pl.semaphore_signal(barrier, inc=1, device_id=dev, device_id_type=MESH)

    for d in (1, 3):
        dev = p.plane((p.x + d) % 4, p.z, 1 - p.c)
        pl.semaphore_signal(barrier, inc=1, device_id=dev, device_id_type=MESH)

    for load in loads[2:]:
        load.start()
    loads[0].wait()
    loads[1].wait()
    @pl.when(jnp.logical_not(p.mover))
    def _():
        xhat, _ = norm(tok[...].astype(F32))
        r.h1[own, :] = (xhat * gain1[...]).astype(BF)
        r.xb[...] = tok[...]

    r.qt[...] = jnp.zeros_like(r.qt)
    r.vt[:, 64:80, :] = jnp.ones((2, 16, T), BF)
    r.mt[FF:FR, :] = jnp.zeros((FR - FF, T), BF)
    r.dat[FF:FR, :] = jnp.zeros((FR - FF, T), BF)
    r.dbt[FF:FR, :] = jnp.zeros((FR - FF, T), BF)
    whole_wo = WholeWeight(p, wout, r.wo, r.s_ag_wo)
    whole_wo.near().start()
    sw_cot = Swap(p, cot, r.cotb.at[own], r.s_sw_cot, r.cotb.at[other])
    sw_cot.start_near()
    pl.semaphore_wait(barrier, 24)

    def sw_x(i):
        half = rows(i * 64, 64)
        sems = r.s_sw_x
        return remote(tok.at[half], r.xb.at[half], sems.at[i], sems.at[2 + i], p.partner())

    def norm_half(i):
        sw_x(i).wait()
        xhat, _ = norm(r.xb[i * 64 : i * 64 + 64, :].astype(F32))
        r.h1[rows(p.me * B + i * 64, 64), :] = (xhat * gain1[...]).astype(BF)

    f_w = Fetch(p, win, r.w, lambda role: rows(role * 128, 128 + role * 128), r.s_f_w)
    f_wg = [
        Fetch(p, wgate.at[i], r.wg.at[i], lambda role: (slice(None), pl.ds(512 * role, 512)), r.s_f_wg.at[i])
        for i in range(2)
    ]
    f_wm = Fetch(p, wmix, r.wm, lambda role: (slice(None), pl.ds(256 * role, 256 + 512 * role)), r.s_f_wm)
    ag_h1, ag_h2, ag_gb = gather(r.h1, "h1"), gather(r.h2, "h2"), gather(r.gb, "gb")
    ag_cot = gather(r.cotb, "cot")

    @pl.when(p.mover)
    def _():
        sw_x(0).start()
        sw_x(1).start()

    f_w.start()
    pl.when(jnp.logical_not(p.mover))(lambda: ag_h1.start())
    whole_wo.w0()
    sw_cot.start_far()
    f_wg[0].start()
    f_wg[1].start()

    @pl.when(p.mover)
    def _():
        norm_half(0)
        ag_h1.start_top()
        norm_half(1)
        ag_h1.start_bottom()

    ag_h1.second()
    whole_wo.w1()
    f_w.wait()
    for load in loads[2:]:
        load.wait()

    def project(yy):
        at = rows(yy * 256, 256)
        lanes = cols(yy * 256, 256)
        u = nt(r.h1[at, :], r.w[...])
        co, si = cosine[at, :], signed[at, :]
        q = u[:, :128]
        q = (q * co + swap_halves(q) * si) * (0.125 * LOG2E)
        r.q[at, :] = q.astype(BF)
        qt = q.T.astype(BF)
        r.qt[0, 0:64, lanes] = qt[0:64]
        r.qt[1, 64:128, lanes] = qt[64:128]
        k = u[:, 128:256]
        k = k * co + swap_halves(k) * si
        r.k[at, :] = k.astype(BF)
        r.kt[:, lanes] = k.T.astype(BF)
        v = u[:, 256:]
        r.v[at, :] = v.astype(BF)
        vt = v.T.astype(BF)
        r.vt[0, 0:64, lanes] = vt[0:64]
        r.vt[1, 0:64, lanes] = vt[64:128]

    def early(step):
        @pl.when(step == 1)
        def _():
            sw_cot.wait()
            ag_cot.start()

        @pl.when(step == 3)
        def _():
            whole_wo.w2()
            f_wm.start()

    ag_h1.steps(project, early, True)

    x_o = Exchange(
        p, lambda j: r.o.at[rows(j * B, B)], r.orow.at[:, own_cols], r.o, r.s_x_o
    )

    @pl.loop(0, 4)
    def _(step):
        yy = (p.y + pick(step, 2, 1, 3, 0)) % 4
        lanes = cols(yy * 256, 256)

        pl.when(step == 3)(whole_wo.w3)
        scores = [nn(r.k[...], r.qt[h, :, lanes]) for h in range(2)]
        parts = []
        for h in range(2):
            probs = jnp.exp2(scores[h] - jnp.max(scores[h], 0, keepdims=True)).astype(BF)
            r.pt[h, :, lanes] = probs
            acc = nn(r.vt[h], probs)
            inverse = 1.0 / acc[64:65]
            r.linv[h, :, lanes] = inverse
            parts.append(acc[0:64] * inverse)
        ot = jnp.concatenate(parts, 0)
        r.ot[:, lanes] = ot
        r.o[rows(yy * 256, 256), :] = ot.T.astype(BF)
        x_o.start_pair(yy)

    r.orow[:, own_cols] = r.o[own, :]
    ag_cot.first()
    ag_cot.second()
    whole_wo.w4()
    x_o.wait()

    x = r.xb[...].astype(F32)
    y1 = x + nn(r.orow[...], r.wo[...])
    r.y1[...] = y1
    xhat, inverse = norm(y1)
    r.xhat2[...] = xhat
    r.inv2[...] = inverse
    r.h2[own, :] = (xhat * gain2[...]).astype(BF)
    ag_h2.start()
    x_o.sent()
    ag_cot.third()
    f_wg[0].wait()
    f_wg[1].wait()
    f_wm.wait()
    ag_cot.rest()

    def mix(yy):
        at = rows(yy * 256, 256)
        lanes = cols(yy * 256, 256)
        h2 = r.h2[at, :]
        a = nt(h2, r.wg[0])
        b = nt(h2, r.wg[1])
        cdf = 0.5 * (1.0 + lax.erf(a * 0.7071067811865476))
        gelu = a * cdf
        slope = cdf + a * (jnp.exp(-0.5 * a * a) * 0.3989422804014327)
        m = gelu * b
        dm = nt(r.cotb[at, :], r.wm[...]).astype(BF).astype(F32)
        da = dm * b * slope
        db = dm * gelu
        r.m[at, :] = m.astype(BF)
        r.da[at, :] = da.astype(BF)
        r.db[at, :] = db.astype(BF)
        r.mt[0:FF, lanes] = m.T.astype(BF)
        r.dat[0:FF, lanes] = da.T.astype(BF)
        r.dbt[0:FF, lanes] = db.T.astype(BF)

    ag_h2.steps(mix)

    def back_mix(yy):
        at = rows(yy * 256, 256)
        return nn(r.da[at, :], r.wg[0]) + nn(r.db[at, :], r.wg[1])

    rs_2 = scatter("r2")
    rs_2.phase(back_mix)
    sums_m = StagedPlaneSum(
        p, r.gm, r.gm_big, r.gm_res, r.gm_small, r.gm_mine, r.gm_out, r.s_sm, r.s_sm_back
    )

    def mix_grads(i):
        lanes = cols(i * 256, 256)
        grads = [
            nn(r.mt[...], r.cotb[:, lanes]).astype(BF),
            nn(r.dat[...], r.h2[:, lanes]).astype(BF),
            nn(r.dbt[...], r.h2[:, lanes]).astype(BF),
            jnp.zeros((1024 - 3 * FR, 256), BF),
        ]
        r.gm[:, :, :, lanes] = jnp.concatenate(grads, 0).reshape(4, 4, 64, 256)

    pl.loop(0, 2)(mix_grads)
    sums_m.first[0].start()
    rs_2.step1()
    pl.loop(2, 4)(mix_grads)
    sums_m.first[1].start()
    dh2 = rs_2.step2()

    dx, dgain2 = norm_back(dh2, r.xhat2[...], r.inv2[...], gain2[...])
    gy = r.cotb[own, :].astype(F32) + dx
    r.gy[...] = gy
    r.gb[own, :] = gy.astype(BF)
    r.dorow[...] = nt(r.gb[own, :], r.wo[...]).astype(BF)
    x_do = Exchange(p, lambda j: r.dorow.at[:, cols(j * B, B)], r.dob.at[own], r.dob, r.s_x_do)
    x_do.start()
    r.dob[own, :] = r.dorow[:, own_cols]
    ag_gb.start()
    gain_2 = Gain(p, r.g2t, r.g2p, r.s_g2)
    gain_2.start(dgain2)
    rs_o = scatter("ro")
    rs_o.phase(lambda yy: nn(r.m[rows(yy * 256, 256), :], r.wm[...]), False)

    @pl.loop(0, 4)
    def _(step):
        yy = (p.y + pick(step, 0, 3, 1, 2)) % 4
        at = rows(yy * 256, 256)
        lanes = cols(yy * 256, 256)
        x_do.wait_pair(yy)
        pl.when(step == 1)(lambda: sums_m.to_second(0))
        dot = r.dob[at, :].astype(F32).T
        zero = jnp.zeros((64, 256), BF)
        scaled = []
        for h in range(2):
            half = dot[h * 64 : h * 64 + 64] * r.linv[h, :, lanes]
            scaled.append(half)
        dpt = [
            nn(r.v[...], jnp.concatenate([scaled[0].astype(BF), zero], 0)),
            nn(r.v[...], jnp.concatenate([zero, scaled[1].astype(BF)], 0)),
        ]
        r.dos[at, :] = jnp.concatenate(scaled, 0).T.astype(BF)
        for h in range(2):
            half = slice(h * 64, h * 64 + 64)
            weighted = jnp.sum(scaled[h] * r.ot[half, lanes], 0, keepdims=True)
            ds = (r.pt[h, :, lanes].astype(F32) * (dpt[h] - weighted)).astype(BF)
            r.ds[h, :, lanes] = ds
            r.dqt[half, lanes] = nn(r.kt[half, :], ds)

    x_do.sent()
    sums_m.to_second(1)

    def back_project(yy):
        at = rows(yy * 256, 256)
        lanes = cols(yy * 256, 256)
        first = lax.broadcasted_iota(jnp.int32, (256, B), 1) < 64
        dk = jnp.where(first, nn(r.ds[0, at, :], r.q[...]), nn(r.ds[1, at, :], r.q[...])) * (1 / LOG2E)
        dv = jnp.where(first, nn(r.pt[0, at, :], r.dos[...]), nn(r.pt[1, at, :], r.dos[...]))
        co, si = cosine[at, :], signed[at, :]
        dq = r.dqt[:, lanes].T * 0.125
        dq = dq * co - swap_halves(dq) * si
        dk = dk * co - swap_halves(dk) * si
        r.dqkvt[0:128, lanes] = dq.T.astype(BF)
        r.dqkvt[128:256, lanes] = dk.T.astype(BF)
        r.dqkvt[256:384, lanes] = dv.T.astype(BF)
        r.dqkv[at, :] = jnp.concatenate([dq.astype(BF), dk.astype(BF), dv.astype(BF)], 1)

    pl.loop(0, 4)(back_project)
    gain_2.middle()

    def spread_out(full, i, off, grad):
        size = grad.shape[0] // 8
        full[:, pl.ds(2 * i, 2), :, off : off + 256] = grad.astype(BF).reshape(4, 2, size, 256)

    sums_a = PlaneSum(
        p, r.ga, r.ga_big, r.ga_res, r.ga_small, r.ga_mine, r.ga_out, r.s_sa, r.s_sa_back
    )
    for n in range(2):

        @pl.loop(0, 2)
        def _(i, off=256 * n):
            spread_out(r.ga, i, off, nn(r.dqkvt[...], r.h1[:, cols(i * 512 + off, 256)]))

        sums_a.first[n].start()

    sums_m.to_mine()
    sums_m.g0()
    ag_gb.first()
    ag_gb.second()
    rs_1 = scatter("r1")

    rs_1.phase(lambda yy: nn(r.dqkv[rows(yy * 256, 256), :], r.w[...]))
    rs_1.step1()
    sums_a.to_second(0, 1)
    sums_m.g1()
    ag_gb.third()
    ag_gb.rest()
    sums_o = PlaneSum(
        p, r.go, r.go_big, r.go_res, r.go_small, r.go_mine, r.go_out, r.s_so, r.s_so_back
    )
    for n in range(2):

        @pl.loop(0, 2)
        def _(i, off=256 * n):
            spread_out(r.go, i, off, nn(r.ot[...].astype(BF), r.gb[:, cols(i * 512 + off, 256)]))

        sums_o.first[n].start()

    rs_o.step0()
    dh1 = rs_1.step2()
    xhat, inverse = norm(r.xb[...].astype(F32))
    dx, dgain1 = norm_back(dh1, xhat, inverse, gain1[...])
    gain_1 = Gain(p, r.g1t, r.g1p, r.s_g1)
    gain_1.start(dgain1)
    rs_o.step_right()
    rs_o.step_left()
    r.tg_here[...] = (r.gy[...] + dx).astype(BF)
    sw_tg = Swap(p, r.tg_here, r.tg_out, r.s_sw_tg)
    sw_tg.start()
    sums_a.to_mine()
    sums_a.give()
    sums_o.to_second(0, 1)
    sums_m.g2()
    gain_1.middle()
    rs_o.step1()
    sums_o.to_mine()
    sums_o.give()
    sums_m.g3()
    r.lo_here[...] = (r.y1[...] + rs_o.step2()).astype(BF)
    sw_lo = Swap(p, r.lo_here, r.lo_out, r.s_sw_lo)
    sw_lo.start()
    sw_tg.wait()
    tg_copy = pltpu.make_async_copy(r.tg_out, tg_ref, r.s_outs.at[0])
    tg_copy.start()
    sums_a.take(ga_ref, r.s_outs.at[3])
    sums_o.take(go_ref, r.s_outs.at[4])
    sums_m.finish()
    gm_copy = pltpu.make_async_copy(r.gm_out, gm_ref, r.s_outs.at[1])
    gm_copy.start()
    sw_lo.wait()
    lo_copy = pltpu.make_async_copy(r.lo_out, lo_ref, r.s_outs.at[2])
    lo_copy.start()
    gains_ref[1:2, :] = gain_2.end()
    gains_ref[0:1, :] = gain_1.end()
    sums_a.taken()
    sums_o.taken()
    for copy in [lo_copy, tg_copy, gm_copy]:
        copy.wait()
    drain(r.ga_out, r.s_outs.at[3])
    drain(r.go_out, r.s_outs.at[4])


def widen(
    lo, tg, ga, go, gm, gains, lo_ref, tg_ref, gi_ref, go_ref, gg_ref, gm_ref, first_ref, second_ref,
    lo_in, tg_in, ga_in, go_in, gm_in, tg_out, ga_out, go_out, gm_out, sems,
):
    def whole(held, wide, first, size):
        wide[first : first + size, :] = held[first : first + size, :].astype(F32)

    def chunks(held, wide, first, size):
        size = size // 8
        for z in range(4):
            for x in range(4):
                group, half = (z * 2 + x % 2) * size, x // 2 * 512
                wide[group : group + size, half : half + 512] = held[z, x].astype(F32)

    targets = gm_ref, gg_ref.at[0], gg_ref.at[1]
    pieces = [(gm, gm_in, gm_out, i * FR, FF, target, whole) for i, target in enumerate(targets)]
    pieces += [
        (ga, ga_in, ga_out, 0, 384, gi_ref, chunks),
        (go, go_in, go_out, 0, B, go_ref, chunks),
        (tg, tg_in, tg_out, 0, B, tg_ref, whole),
    ]
    loads, stores = [], []
    for i, (src, held, _, first, size, _, _) in enumerate(pieces):
        if size == FF:
            src, held = src.at[pl.ds(first, FR)], held.at[pl.ds(first, FR)]
        loads.append(pltpu.make_async_copy(src, held, sems.at[i]))
    loads.append(pltpu.make_async_copy(lo, lo_in, sems.at[6]))
    for load in loads:
        load.start()
    for i in range(8):
        first_ref[i : i + 1, :] = gains[0:1, i * B : i * B + B]
        second_ref[i : i + 1, :] = gains[1:2, i * B : i * B + B]
    for i, (_, held, wide, first, size, target, convert) in enumerate(pieces):
        loads[i].wait()
        convert(held, wide, first, size)
        stores.append(pltpu.make_async_copy(wide.at[pl.ds(first, size)], target, sems.at[7 + i]))
        stores[-1].start()
    loads[6].wait()
    stores.append(pltpu.make_async_copy(lo_in, lo_ref, sems.at[13]))
    stores[-1].start()
    for store in stores:
        store.wait()


def local(tokens, attn_in, attn_out, mlp_in, mlp_out, norm_first, norm_second, cotangent):
    cosine, signed = tables()
    any_space = pl.BlockSpec(memory_space=pl.ANY)
    vmem = pl.BlockSpec(memory_space=pltpu.VMEM)
    limit = 63 * 1024 * 1024
    shapes = [(B, D), (B, D), (4, 4, 48, 512), (4, 4, 16, 512), (4, 4, 64, D)]
    lo, tg, ga, go, gm, gains = pl.pallas_call(
        kernel,
        out_shape=tuple(jax.ShapeDtypeStruct(shape, BF) for shape in shapes)
        + (jax.ShapeDtypeStruct((2, D), F32),),
        in_specs=[any_space] * 10,
        out_specs=(any_space,) * 5 + (vmem,),
        scratch_shapes=[pltpu.VMEM(shape, kind) for shape, kind in SCRATCH.values()]
        + [pltpu.SemaphoreType.DMA(shape) for shape in SEMS.values()],
        compiler_params=pltpu.CompilerParams(
            collective_id=0, has_side_effects=True, vmem_limit_bytes=limit
        ),
    )(
        tokens,
        cotangent,
        attn_in.transpose(1, 2, 3, 0).reshape(384, D),
        attn_out.reshape(B, D),
        mlp_in.transpose(0, 2, 1),
        mlp_out,
        norm_first.reshape(1, D),
        norm_second.reshape(1, D),
        jnp.asarray(cosine),
        jnp.asarray(signed),
    )
    wide = [(B, D), (384, D), (B, D), (2, FF, D), (FF, D), (8, B), (8, B)]
    lo, tg, gi, go, gg, gm, first, second = pl.pallas_call(
        widen,
        out_shape=(jax.ShapeDtypeStruct((B, D), BF),)
        + tuple(jax.ShapeDtypeStruct(shape, F32) for shape in wide),
        in_specs=[any_space] * 5 + [vmem],
        out_specs=(any_space,) * 6 + (vmem, vmem),
        scratch_shapes=[
            pltpu.VMEM((B, D), BF),
            pltpu.VMEM((B, D), BF),
            pltpu.VMEM((4, 4, 48, 512), BF),
            pltpu.VMEM((4, 4, 16, 512), BF),
            pltpu.VMEM((1024, D), BF),
            pltpu.VMEM((B, D), F32),
            pltpu.VMEM((384, D), F32),
            pltpu.VMEM((B, D), F32),
            pltpu.VMEM((3 * FR, D), F32),
            pltpu.SemaphoreType.DMA((14,)),
        ],
        compiler_params=pltpu.CompilerParams(vmem_limit_bytes=limit),
    )(lo, tg, ga, go, gm.reshape(1024, D), gains)
    return (
        lo,
        tg,
        gi.reshape(3, 2, 64, D).transpose(3, 0, 1, 2),
        go.reshape(2, 64, D),
        gg.transpose(0, 2, 1),
        gm,
        first.reshape(D),
        second.reshape(D),
    )


def solution(mesh):
    placed = (
        P(("dp", "tensor"), None),
        P(None, None, "tensor", None),
        P("tensor", None, None),
        P(None, None, "tensor"),
        P("tensor", None),
        P(),
        P(),
        P(("dp", "tensor"), None),
    )
    return jax.shard_map(
        local,
        mesh=mesh,
        in_specs=placed,
        out_specs=(
            P(("dp", "tensor"), None),
            P(("dp", "tensor"), None),
            P(None, None, "tensor", None),
            P("tensor", None, None),
            P(None, None, "tensor"),
            P("tensor", None),
            P(),
            P(),
        ),
        check_vma=False,
    )
```

```python
import jax
import jax.numpy as jnp
import numpy as np
from jax import lax
from jax.experimental import pallas as pl
from jax.experimental.pallas import tpu as pltpu
from jax.sharding import PartitionSpec as P

MESH = pl.DeviceIdType.MESH
BF = jnp.bfloat16
F32 = jnp.float32
EPS = 1e-05
THETA = 160000.0
T = 1024
D = 1024
B = 128
FF = 328
FR = 336
LOG2E = 1.4426950408889634


def tables():
    places = np.arange(T, dtype=np.float32)
    frequency = (THETA ** (-np.arange(0, 64, 2, dtype=np.float32) / 64)).astype(np.float32)
    angles = places[:, None] * frequency[None, :]
    cosine, sine = np.cos(angles), np.sin(angles)
    cosine = np.concatenate([cosine, cosine] * 2, -1)
    signed = np.concatenate([-sine, sine] * 2, -1)
    order = np.concatenate([np.arange(B) + ((j % 2) * 4 + j // 2) * B for j in range(8)])
    return cosine[order].astype(np.float32), signed[order].astype(np.float32)


def nn(a, b):
    return jnp.dot(a, b, preferred_element_type=F32)


def nt(a, b):
    return lax.dot_general(a, b, (((1,), (1,)), ((), ())), preferred_element_type=F32)


def pick(step, a, b, c, d):
    return jnp.where(step == 0, a, jnp.where(step == 1, b, jnp.where(step == 2, c, d)))


def swap_halves(u):
    lane = lax.broadcasted_iota(jnp.int32, u.shape, 1)
    return jnp.where((lane % 64) < 32, pltpu.roll(u, 96, 1), pltpu.roll(u, 32, 1))


def norm(v):
    centred = v - jnp.mean(v, -1, keepdims=True)
    inverse = lax.rsqrt(jnp.mean(centred * centred, -1, keepdims=True) + EPS)
    return centred * inverse, inverse


def norm_back(gradient, xhat, inverse, gain):
    e = gradient * gain
    dx = inverse * (
        e - jnp.mean(e, -1, keepdims=True) - xhat * jnp.mean(e * xhat, -1, keepdims=True)
    )
    return dx, jnp.sum(gradient * xhat, 0, keepdims=True)


def rows(start, size):
    return pl.ds(pl.multiple_of(start, 16), size)


def cols(start, size):
    return pl.ds(pl.multiple_of(start, 128), size)


def remote(src, dst, ssem, rsem, dev):
    return pltpu.make_async_remote_copy(
        src_ref=src, dst_ref=dst, send_sem=ssem, recv_sem=rsem, device_id=dev, device_id_type=MESH
    )


def drain(ref, sem):
    pltpu.make_async_copy(ref, ref, sem).wait()


class Place:
    def __init__(self):
        dp, tensor = lax.axis_index("dp"), lax.axis_index("tensor")
        self.dp, self.tensor = dp, tensor
        self.c = dp % 2
        self.xlo, self.y = tensor // 4, tensor % 4
        self.z = dp // 4
        self.x = ((dp // 2) % 2) * 2 + self.xlo
        self.me = 2 * self.y + self.c
        self.mover = self.c != self.xlo
        self.right, self.left = (self.y + 1) % 4, (self.y + 3) % 4
        self.opp = (self.y + 2) % 4

    def team(self, core, y):
        return {"dp": self.dp - self.c + core, "tensor": self.xlo * 4 + y}

    def plane(self, x, z, core=None):
        core = self.c if core is None else core
        return {"dp": z * 4 + (x // 2) * 2 + core, "tensor": (x % 2) * 4 + self.y}

    def partner(self):
        return {"dp": self.dp - self.c + self.xlo, "tensor": self.c * 4 + self.y}


class Gather:
    def __init__(self, place, buf, sems):
        self.p, self.buf, self.sems = place, buf, sems

    def msg(self, i):
        p = self.p
        me, lt, rt, op = p.me, 2 * p.left + p.c, 2 * p.right + p.c, 2 * p.opp + p.c
        right, left = p.team(p.c, p.right), p.team(p.c, p.left)
        sib = p.team(1 - p.c, p.y)
        block, first, size, dev = (
            (me, 0, 64, right),
            (me, 64, 64, left),
            (me, 64, 64, right),
            (me, 0, 64, left),
            (me, 0, 128, sib),
            (lt, 0, 64, right),
            (rt, 64, 64, left),
            (lt, 0, 128, sib),
            (rt, 0, 128, sib),
            (op, 0, 64, sib),
            (op, 64, 64, sib),
        )[i]
        ref = self.buf.at[rows(block * B + first, size)]
        return remote(ref, ref, self.sems.at[11], self.sems.at[i], dev)

    def start(self):
        for i in range(5):
            self.msg(i).start()

    def start_top(self):
        self.msg(0).start()
        self.msg(3).start()

    def start_bottom(self):
        self.msg(1).start()
        self.msg(2).start()
        self.msg(4).start()

    def first(self):
        self.msg(4).wait_recv()

    def second(self):
        self.msg(0).wait_recv()
        self.msg(5).start()
        self.msg(1).wait_recv()
        self.msg(6).start()
        self.msg(2).wait_recv()
        self.msg(7).start()
        self.msg(3).wait_recv()
        self.msg(8).start()

    def third(self):
        self.msg(5).wait_recv()
        self.msg(9).start()
        self.msg(6).wait_recv()
        self.msg(10).start()

    def left_in(self):
        self.msg(7).wait_recv()

    def right_in(self):
        self.msg(8).wait_recv()

    def opp_in(self):
        self.msg(9).wait_recv()
        self.msg(10).wait_recv()

    def sent(self):
        drain(self.buf.at[pl.ds(0, 896)], self.sems.at[11])

    def rest(self):
        self.left_in()
        self.right_in()
        self.opp_in()
        self.sent()

    def steps(self, body, hook=None, forwarded=False, idle=None):
        p = self.p

        @pl.loop(0, 4)
        def _(step):
            @pl.when(step == 0)
            def _():
                self.first()

            @pl.when(step == 1)
            def _():
                if idle is not None:
                    idle()
                if not forwarded:
                    self.second()
                self.left_in()

            @pl.when(step == 2)
            def _():
                self.right_in()

            @pl.when(step == 3)
            def _():
                self.third()
                self.opp_in()

            if hook is not None:
                hook(step)
            body((p.y + pick(step, 0, 3, 1, 2)) % 4)

        self.sent()


class Scatter:
    def __init__(self, place, part, got, held, top, bottom, from_left, from_right, sems):
        self.p = place
        self.part, self.got, self.held = part, got, held
        self.top, self.bottom = top, bottom
        self.from_left, self.from_right = from_left, from_right
        self.sems = sems

    def off(self, step):
        return pick(step, 2, 1, 3, 0)

    def sib(self, step):
        p = self.p
        yy = (p.y + self.off(step)) % 4
        return remote(
            self.part.at[rows((2 * yy + 1 - p.c) * B, B)],
            self.got.at[rows(yy * B, B)],
            self.sems.at[10],
            self.sems.at[step],
            p.team(1 - p.c, p.y),
        )

    def msg(self, i):
        p = self.p
        right, left = p.team(p.c, p.right), p.team(p.c, p.left)
        block, first, dst, dev = (
            (p.opp, 0, self.top, right),
            (p.opp, 64, self.bottom, left),
            (p.right, 64, self.from_left.at[rows(64, 64)], right),
            (p.right, 0, self.from_left.at[rows(0, 64)], right),
            (p.left, 0, self.from_right.at[rows(0, 64)], left),
            (p.left, 64, self.from_right.at[rows(64, 64)], left),
        )[i]
        return remote(
            self.held.at[rows(block * B + first, 64)], dst, self.sems.at[10], self.sems.at[4 + i], dev
        )

    def phase(self, compute, early=True, hook=None):
        p = self.p

        @pl.loop(0, 4)
        def _(step):
            yy = (p.y + self.off(step)) % 4
            self.part[rows(yy * 256, 256), :] = compute(yy).astype(BF)
            self.sib(step).start()
            if early:
                pl.when(step == 1)(self.step0)
                pl.when(step == 2)(self.step_right)
                pl.when(step == 3)(self.step_left)
            if hook is not None:
                hook(step)

    def pair_sum(self, yy):
        own = self.part[rows((2 * yy + self.p.c) * B, B), :].astype(F32)
        return own + self.got[rows(yy * B, B), :].astype(F32)

    def step0(self):
        p = self.p
        self.sib(0).wait_recv()
        self.held[rows(p.opp * B, B), :] = self.pair_sum(p.opp).astype(BF)
        self.msg(0).start()
        self.msg(1).start()

    def step_right(self):
        p = self.p
        self.sib(1).wait_recv()
        self.held[rows(p.right * B, B), :] = self.pair_sum(p.right).astype(BF)
        self.msg(2).start()

    def step_left(self):
        p = self.p
        self.sib(2).wait_recv()
        self.held[rows(p.left * B, B), :] = self.pair_sum(p.left).astype(BF)
        self.msg(4).start()

    def step1(self):
        p = self.p
        top, bottom = rows(p.right * B, 64), rows(p.left * B + 64, 64)
        self.msg(0).wait_recv()
        self.held[top, :] = (self.held[top, :].astype(F32) + self.top[...].astype(F32)).astype(BF)
        self.msg(3).start()
        self.msg(1).wait_recv()
        self.held[bottom, :] = (
            self.held[bottom, :].astype(F32) + self.bottom[...].astype(F32)
        ).astype(BF)
        self.msg(5).start()

    def step2(self):
        p = self.p
        self.sib(3).wait_recv()
        total = self.pair_sum(p.y)
        for i in range(2, 6):
            self.msg(i).wait_recv()
        total = total + self.from_left[...].astype(F32) + self.from_right[...].astype(F32)
        drain(self.part.at[pl.ds(0, 896)], self.sems.at[10])
        return total


class Gain:
    def __init__(self, place, team_buf, plane_buf, sems):
        self.p, self.team_buf, self.plane_buf, self.sems = place, team_buf, plane_buf, sems

    def start(self, value):
        p = self.p
        ref = self.team_buf.at[p.me]
        ref[...] = value

        @pl.loop(1, 8)
        def _(k):
            j = (p.me + k) % 8
            remote(ref, ref, self.sems.at[0], self.sems.at[1], p.team(j % 2, j // 2)).start()

    def middle(self):
        p = self.p
        drain(self.team_buf.at[pl.ds(0, 7)], self.sems.at[1])
        ref = self.plane_buf.at[p.z * 4 + p.x]
        ref[...] = jnp.sum(self.team_buf[...], 0)

        @pl.loop(1, 16)
        def _(k):
            dev = p.plane((p.x + k % 4) % 4, (p.z + k // 4) % 4)
            remote(ref, ref, self.sems.at[2], self.sems.at[3], dev).start()

        drain(self.team_buf.at[pl.ds(0, 7)], self.sems.at[0])

    def end(self):
        drain(self.plane_buf.at[pl.ds(0, 15)], self.sems.at[3])
        total = jnp.sum(self.plane_buf[...], 0)
        drain(self.plane_buf.at[pl.ds(0, 15)], self.sems.at[2])
        return total


class Swap:
    def __init__(self, place, src, dst, sems, there=None):
        self.p, self.src, self.dst, self.sems = place, src, dst, sems
        self.there = dst if there is None else there

    def far(self):
        return remote(self.src, self.there, self.sems.at[0], self.sems.at[1], self.p.partner())

    def near(self):
        return pltpu.make_async_copy(self.src, self.dst, self.sems.at[2])

    def start(self):
        self.start_far()
        self.start_near()

    def start_far(self):
        pl.when(self.p.mover)(lambda: self.far().start())

    def start_near(self):
        pl.when(jnp.logical_not(self.p.mover))(lambda: self.near().start())

    def wait(self):
        pl.when(self.p.mover)(lambda: self.far().wait())
        pl.when(jnp.logical_not(self.p.mover))(lambda: self.near().wait())


class Fetch:
    def __init__(self, place, src, dst, part, sems):
        self.p, self.src, self.dst, self.part, self.sems = place, src, dst, part, sems

    def far(self, role):
        p = self.p
        step = 1 + 2 * ((p.x + role) % 2)
        part = self.part(role)
        return remote(
            self.src.at[part],
            self.dst.at[part],
            self.sems.at[role],
            self.sems.at[2 + role],
            p.plane((p.x + step) % 4, p.z, p.xlo),
        )

    def near(self):
        return pltpu.make_async_copy(self.src, self.dst, self.sems.at[4])

    def start(self):
        self.start_away()
        self.start_partner()

    def start_away(self):
        pl.when(self.p.mover)(lambda: self.far(1).start())
        pl.when(jnp.logical_not(self.p.mover))(lambda: self.near().start())

    def start_partner(self):
        pl.when(self.p.mover)(lambda: self.far(0).start())

    def wait(self):
        @pl.when(self.p.mover)
        def _():
            self.far(0).wait()
            self.far(1).wait()

        pl.when(jnp.logical_not(self.p.mover))(lambda: self.near().wait())


class WholeWeight:
    def __init__(self, place, src, buf, sems):
        self.p, self.src, self.buf, self.sems = place, src, buf, sems

    def near(self):
        p = self.p
        return pltpu.make_async_copy(
            self.src, self.buf.at[rows((2 * p.y + p.xlo) * B, B)], self.sems.at[18]
        )

    def msg(self, i):
        p = self.p
        right, left = p.team(p.c, p.right), p.team(p.c, p.left)
        sib = p.team(1 - p.c, p.y)
        side = p.plane((p.x + 1 + 2 * p.c) % 4, p.z)
        ys = (p.y, p.left, p.right, p.opp)
        first, size = 0, 64
        if i < 6:
            y, first, size, dev = (
                (p.y, 0, 32, right),
                (p.y, 32, 32, left),
                (p.y, 32, 32, right),
                (p.y, 0, 32, left),
                (p.left, 0, 32, right),
                (p.right, 32, 32, left),
            )[i]
            group = p.xlo
        elif i < 10:
            y, group, dev = ys[i - 6], p.xlo, side
        elif i < 13:
            y, group, dev = ys[i - 9], p.xlo, sib
        else:
            y, group, dev = ys[i - 13], 1 - p.xlo, sib
        ref = self.buf.at[rows((2 * y + group) * B + p.c * 64 + first, size)]
        return remote(ref, ref, self.sems.at[17], self.sems.at[i], dev)

    def go(self, *which):
        for i in which:
            self.msg(i).start()

    def got(self, *which):
        for i in which:
            self.msg(i).wait_recv()

    def w0(self):
        self.near().wait()
        self.go(0, 1, 2, 3)

    def w1(self):
        self.go(6)
        self.got(0)
        self.go(4)
        self.got(1)
        self.go(5)
        self.got(2)
        self.go(7, 10)
        self.got(3)
        self.go(8, 11)

    def w2(self):
        self.got(4, 5)
        self.go(9, 12)

    def w3(self):
        for i in range(4):
            self.got(6 + i)
            self.go(13 + i)

    def w4(self):
        self.got(*range(10, 17))
        drain(self.buf.at[pl.ds(0, 896)], self.sems.at[17])


class AxisSum:
    def __init__(self, i, dev, blk, bufs, sems):
        self.i, self.dev, self.blk, self.bufs, self.sems = i, dev, blk, bufs, sems

    def start(self):
        for k in (2, 1, 3):
            j = (self.i + k) % 4
            remote(
                self.blk(j), self.bufs.at[k - 1], self.sems.at[1], self.sems.at[0], self.dev(j)
            ).start()

    def total(self):
        drain(self.bufs, self.sems.at[0])
        total = self.blk(self.i)[...].astype(F32)
        for k in range(3):
            total = total + self.bufs[k].astype(F32)
        return total.astype(BF)

    def sent(self):
        drain(self.bufs, self.sems.at[1])


class PlaneSum:
    def __init__(self, place, full, big, res, small, mine, out, sems, back):
        p = self.p = place
        self.full, self.mine, self.out, self.back, self.res = full, mine, out, back, res
        along_z = p.z, lambda j: p.plane(p.x, j)
        along_x = p.x, lambda j: p.plane(j, p.z)
        self.half = half = full.shape[3] // 2
        self.first = (
            AxisSum(*along_z, lambda j: full.at[j, :, :, pl.ds(0, half)], big.at[0], sems.at[0]),
            AxisSum(*along_x, lambda j: full.at[:, j, :, pl.ds(half, half)], big.at[1], sems.at[1]),
        )
        self.second = (
            AxisSum(*along_x, lambda j: res.at[0, j], small.at[0], sems.at[2]),
            AxisSum(*along_z, lambda j: res.at[1, j], small.at[1], sems.at[3]),
        )

    def to_second(self, *which):
        for n in which:
            self.res[n] = self.first[n].total()
            self.second[n].start()

    def to_mine(self):
        for n in range(2):
            self.mine[:, n * self.half : (n + 1) * self.half] = self.second[n].total()

    def give_msg(self, k):
        p = self.p
        dev = p.plane((p.x + k % 4) % 4, (p.z + k // 4) % 4)
        ref = self.out.at[p.z, p.x]
        return remote(self.mine, ref, self.back.at[0], self.back.at[2 + k // 4], dev)

    def give(self):
        p = self.p

        @pl.loop(0, 8)
        def _(i):
            k = (i // 2) * 4 + (i % 2) * 2 + jnp.where(p.mover, 1, 0)
            pl.when(k != 0)(lambda: self.give_msg(k).start())

        @self.stays
        def _():
            self.out[p.z, p.x] = self.mine[...]

    def forward(self, i):
        p = self.p
        block = self.out.at[(p.z + 4 - i) % 4]
        return remote(block, block, self.back.at[1], self.back.at[6 + i], p.team(1 - p.c, p.y))

    def to(self, i, target, sem):
        block = (self.p.z + 4 - i) % 4
        return pltpu.make_async_copy(self.out.at[block], target.at[block], sem)

    def take(self, target, sem):
        @self.stays
        def _():
            for i in range(4):
                drain(self.out.at[0, pl.ds(0, 4 if i else 3)], self.back.at[2 + i])
                self.forward(i).start()
                self.to(i, target, sem).start()

        @pl.when(self.p.mover)
        def _():
            for i in range(4):
                self.forward(i).wait_recv()
                self.to(i, target, sem).start()

    def taken(self):
        @pl.when(self.p.mover)
        def _():
            drain(self.out.at[pl.ds(0, 2)], self.back.at[0])

        @self.stays
        def _():
            drain(self.out, self.back.at[1])
            drain(self.full.at[0], self.back.at[0])
            drain(self.full.at[1, pl.ds(0, 3)], self.back.at[0])

        for axis in self.first + self.second:
            axis.sent()

    def stays(self, body):
        pl.when(jnp.logical_not(self.p.mover))(body)


class StagedPlaneSum(PlaneSum):
    def side(self, i):
        p = self.p
        return remote(
            self.mine,
            self.out.at[p.z, p.x],
            self.back.at[15],
            self.back.at[11 + i],
            p.plane((p.x + (1, 3, 2)[i]) % 4, p.z),
        )

    def msg(self, i):
        p = self.p
        lt, rt, op = (p.z + 3) % 4, (p.z + 1) % 4, (p.z + 2) % 4
        right, left, sib = p.plane(p.x, rt), p.plane(p.x, lt), p.team(1 - p.c, p.y)
        block, first, size, dev = (
            (p.z, 0, 2, right),
            (p.z, 2, 2, left),
            (p.z, 2, 2, right),
            (p.z, 0, 2, left),
            (p.z, 0, 4, sib),
            (lt, 0, 2, right),
            (rt, 2, 2, left),
            (lt, 0, 4, sib),
            (rt, 0, 4, sib),
            (op, 0, 2, sib),
            (op, 2, 2, sib),
        )[i]
        ref = self.out.at[block, pl.ds(first, size)]
        return remote(ref, ref, self.back.at[14], self.back.at[i], dev)

    def g0(self):
        p = self.p

        @pl.when(p.mover)
        def _():
            self.side(0).start()
            self.side(1).start()

        @pl.when(jnp.logical_not(p.mover))
        def _():
            self.side(2).start()
            self.out[p.z, p.x] = self.mine[...]

    def g1(self):
        @self.stays
        def _():
            for i in range(3):
                self.side(i).wait_recv()
            for i in range(5):
                self.msg(i).start()

    def g2(self):
        @self.stays
        def _():
            for i in range(4):
                self.msg(i).wait_recv()
                self.msg((5, 6, 7, 8)[i]).start()

    def g3(self):
        @self.stays
        def _():
            for i in (5, 6):
                self.msg(i).wait_recv()
                self.msg(4 + i).start()

    def finish(self):
        @pl.when(self.p.mover)
        def _():
            for i in (4, 7, 8, 9, 10):
                self.msg(i).wait_recv()
            drain(self.full.at[0, pl.ds(0, 2)], self.back.at[15])

        @self.stays
        def _():
            drain(self.mine, self.back.at[15])
            drain(self.out, self.back.at[14])
            drain(self.out.at[pl.ds(0, 3)], self.back.at[14])

        for axis in self.first + self.second:
            axis.sent()


class Exchange:
    def __init__(self, place, src_of, dst, everything, sems):
        self.p, self.src_of, self.dst, self.all, self.sems = place, src_of, dst, everything, sems

    def msg(self, k):
        p = self.p
        j = (p.me + k) % 8
        return remote(
            self.src_of(j), self.dst, self.sems.at[0], self.sems.at[k], p.team(j % 2, j // 2)
        )

    def start_pair(self, yy):
        for core in range(2):
            k = (2 * yy + core + 8 - self.p.me) % 8
            pl.when(k != 0)(lambda: self.msg(k).start())

    def wait(self):
        @pl.loop(1, 8)
        def _(k):
            self.msg(k).wait_recv()

    def wait_pair(self, yy):
        for core in range(2):
            k = (self.p.me + 8 - (2 * yy + core)) % 8
            pl.when(k != 0)(lambda: self.msg(k).wait_recv())

    def start(self):
        @pl.loop(1, 8)
        def _(k):
            self.msg(k).start()

    def sent(self):
        drain(self.all.at[pl.ds(0, 896)], self.sems.at[0])


SCRATCH = dict(
    tok=((B, D), BF),
    gain1=((1, D), F32),
    gain2=((1, D), F32),
    cosine=((T, B), F32),
    signed=((T, B), F32),
    xb=((B, D), BF),
    cotb=((T, D), BF),
    w=((384, D), BF),
    wo=((T, D), BF),
    wg=((2, FF, D), BF),
    wm=((FF, D), BF),
    h1=((T, D), BF),
    h2=((T, D), BF),
    gb=((T, D), BF),
    y1=((B, D), F32),
    xhat2=((B, D), F32),
    inv2=((B, 1), F32),
    gy=((B, D), F32),
    q=((T, B), BF),
    dqkv=((T, 384), BF),
    qt=((2, B, T), BF),
    k=((T, B), BF),
    kt=((B, T), BF),
    v=((T, B), BF),
    vt=((2, 80, T), BF),
    pt=((2, T, T), BF),
    linv=((2, 1, T), F32),
    ot=((B, T), F32),
    o=((T, B), BF),
    orow=((B, D), BF),
    dos=((T, B), BF),
    ds=((2, T, T), BF),
    dqt=((B, T), F32),
    dqkvt=((384, T), BF),
    m=((T, FF), BF),
    da=((T, FF), BF),
    db=((T, FF), BF),
    mt=((FR, T), BF),
    dat=((FR, T), BF),
    dbt=((FR, T), BF),
    gm=((4, 4, 64, D), BF),
    gm_big=((2, 3, 4, 64, 512), BF),
    gm_res=((2, 4, 64, 512), BF),
    gm_small=((2, 3, 64, 512), BF),
    gm_mine=((64, D), BF),
    gm_out=((4, 4, 64, D), BF),
    ga=((4, 4, 48, 512), BF),
    ga_big=((2, 3, 4, 48, 256), BF),
    ga_res=((2, 4, 48, 256), BF),
    ga_small=((2, 3, 48, 256), BF),
    ga_mine=((48, 512), BF),
    ga_out=((4, 4, 48, 512), BF),
    go=((4, 4, 16, 512), BF),
    go_big=((2, 3, 4, 16, 256), BF),
    go_res=((2, 4, 16, 256), BF),
    go_small=((2, 3, 16, 256), BF),
    go_mine=((16, 512), BF),
    go_out=((4, 4, 16, 512), BF),
    dorow=((B, D), BF),
    dob=((T, B), BF),
    g1t=((8, 1, D), F32),
    g1p=((16, 1, D), F32),
    g2t=((8, 1, D), F32),
    g2p=((16, 1, D), F32),
    lo_here=((B, D), BF),
    lo_out=((B, D), BF),
    tg_here=((B, D), BF),
    tg_out=((B, D), BF),
)
for _name in ("r2", "ro", "r1"):
    SCRATCH.update(
        {
            _name + "_got": ((512, D), BF),
            _name + "_held": ((512, D), BF),
            _name + "_top": ((64, D), BF),
            _name + "_bottom": ((64, D), BF),
            _name + "_left": ((B, D), BF),
            _name + "_right": ((B, D), BF),
        }
    )
SCRATCH["r2_part"] = ((T, D), BF)
SEMS = dict(
    ag_h1=(12,), ag_wo=(19,), ag_cot=(12,), ag_h2=(12,), ag_gb=(12,),
    rs_r2=(11,), rs_ro=(11,), rs_r1=(11,),
    sm=(4, 2), sm_back=(16,), sa=(4, 2), sa_back=(10,), so=(4, 2), so_back=(10,), g1=(4,), g2=(4,),
    sw_x=(4,), sw_cot=(3,), sw_lo=(3,), sw_tg=(3,),
    f_w=(5,), f_wg=(2, 5), f_wm=(5,), x_o=(8,), x_do=(8,), outs=(5,), loads=(5,),
)


def kernel(
    tok_in, cot, win, wout, wgate, wmix, gain1_in, gain2_in, cosine_in, signed_in,
    lo_ref, tg_ref, ga_ref, go_ref, gm_ref, gains_ref, *scratch
):
    names = list(SCRATCH) + ["s_" + n for n in SEMS]
    s = dict(zip(names, scratch, strict=True))
    p = Place()

    class R:
        pass

    r = R()
    r.__dict__.update(s)
    tok, gain1, gain2, cosine, signed = r.tok, r.gain1, r.gain2, r.cosine, r.signed
    loads = [
        pltpu.make_async_copy(src, dst, r.s_loads.at[i])
        for i, (src, dst) in enumerate(
            ((tok_in, tok), (gain1_in, gain1), (cosine_in, cosine), (signed_in, signed), (gain2_in, gain2))
        )
    ]
    loads[0].start()
    loads[1].start()
    own = rows(p.me * B, B)
    other = rows((2 * p.y + 1 - p.c) * B, B)
    own_cols = cols(p.me * B, B)

    def gather(buf, name):
        return Gather(p, buf, s["s_ag_" + name])

    def scatter(name):
        part = r.h2 if name == "r1" else r.r2_part
        parts = [s[name + "_" + n] for n in ("got", "held", "top", "bottom", "left", "right")]
        return Scatter(p, part, *parts, s["s_rs_" + name])

    barrier = pltpu.get_barrier_semaphore()

    @pl.loop(1, 8)
    def _(k):
        j = (p.me + k) % 8
        pl.semaphore_signal(barrier, inc=1, device_id=p.team(j % 2, j // 2), device_id_type=MESH)

    @pl.loop(1, 16)
    def _(k):
        dev = p.plane((p.x + k % 4) % 4, (p.z + k // 4) % 4)
        pl.semaphore_signal(barrier, inc=1, device_id=dev, device_id_type=MESH)

    for d in (1, 3):
        dev = p.plane((p.x + d) % 4, p.z, 1 - p.c)
        pl.semaphore_signal(barrier, inc=1, device_id=dev, device_id_type=MESH)

    for load in loads[2:]:
        load.start()
    loads[0].wait()
    loads[1].wait()
    @pl.when(jnp.logical_not(p.mover))
    def _():
        xhat, _ = norm(tok[...].astype(F32))
        r.h1[own, :] = (xhat * gain1[...]).astype(BF)
        r.xb[...] = tok[...]

    r.qt[...] = jnp.zeros_like(r.qt)
    r.vt[:, 64:80, :] = jnp.ones((2, 16, T), BF)
    r.mt[FF:FR, :] = jnp.zeros((FR - FF, T), BF)
    r.dat[FF:FR, :] = jnp.zeros((FR - FF, T), BF)
    r.dbt[FF:FR, :] = jnp.zeros((FR - FF, T), BF)
    whole_wo = WholeWeight(p, wout, r.wo, r.s_ag_wo)
    whole_wo.near().start()
    sw_cot = Swap(p, cot, r.cotb.at[own], r.s_sw_cot, r.cotb.at[other])
    sw_cot.start_near()
    pl.semaphore_wait(barrier, 24)

    def sw_x(i):
        half = rows(i * 64, 64)
        sems = r.s_sw_x
        return remote(tok.at[half], r.xb.at[half], sems.at[i], sems.at[2 + i], p.partner())

    def norm_half(i):
        sw_x(i).wait()
        xhat, _ = norm(r.xb[i * 64 : i * 64 + 64, :].astype(F32))
        r.h1[rows(p.me * B + i * 64, 64), :] = (xhat * gain1[...]).astype(BF)

    f_w = Fetch(p, win, r.w, lambda role: rows(role * 128, 128 + role * 128), r.s_f_w)
    f_wg = [
        Fetch(p, wgate.at[i], r.wg.at[i], lambda role: (slice(None), pl.ds(512 * role, 512)), r.s_f_wg.at[i])
        for i in range(2)
    ]
    f_wm = Fetch(p, wmix, r.wm, lambda role: (slice(None), pl.ds(256 * role, 256 + 512 * role)), r.s_f_wm)
    ag_h1, ag_h2, ag_gb = gather(r.h1, "h1"), gather(r.h2, "h2"), gather(r.gb, "gb")
    ag_cot = gather(r.cotb, "cot")

    @pl.when(p.mover)
    def _():
        sw_x(0).start()
        sw_x(1).start()

    f_w.start()
    pl.when(jnp.logical_not(p.mover))(lambda: ag_h1.start())
    whole_wo.w0()
    sw_cot.start_far()
    f_wg[0].start()
    f_wg[1].start()

    @pl.when(p.mover)
    def _():
        norm_half(0)
        ag_h1.start_top()
        norm_half(1)
        ag_h1.start_bottom()

    ag_h1.second()
    whole_wo.w1()
    f_w.wait()
    for load in loads[2:]:
        load.wait()

    def project(yy):
        at = rows(yy * 256, 256)
        lanes = cols(yy * 256, 256)
        u = nt(r.h1[at, :], r.w[...])
        co, si = cosine[at, :], signed[at, :]
        q = u[:, :128]
        q = (q * co + swap_halves(q) * si) * (0.125 * LOG2E)
        r.q[at, :] = q.astype(BF)
        qt = q.T.astype(BF)
        r.qt[0, 0:64, lanes] = qt[0:64]
        r.qt[1, 64:128, lanes] = qt[64:128]
        k = u[:, 128:256]
        k = k * co + swap_halves(k) * si
        r.k[at, :] = k.astype(BF)
        r.kt[:, lanes] = k.T.astype(BF)
        v = u[:, 256:]
        r.v[at, :] = v.astype(BF)
        vt = v.T.astype(BF)
        r.vt[0, 0:64, lanes] = vt[0:64]
        r.vt[1, 0:64, lanes] = vt[64:128]

    def early(step):
        @pl.when(step == 1)
        def _():
            sw_cot.wait()
            ag_cot.start()

        @pl.when(step == 3)
        def _():
            whole_wo.w2()
            f_wm.start()

    ag_h1.steps(project, early, True)

    x_o = Exchange(
        p, lambda j: r.o.at[rows(j * B, B)], r.orow.at[:, own_cols], r.o, r.s_x_o
    )

    @pl.loop(0, 4)
    def _(step):
        yy = (p.y + pick(step, 2, 1, 3, 0)) % 4
        lanes = cols(yy * 256, 256)

        pl.when(step == 3)(whole_wo.w3)
        scores = [nn(r.k[...], r.qt[h, :, lanes]) for h in range(2)]
        parts = []
        for h in range(2):
            probs = jnp.exp2(scores[h] - jnp.max(scores[h], 0, keepdims=True)).astype(BF)
            r.pt[h, :, lanes] = probs
            acc = nn(r.vt[h], probs)
            inverse = 1.0 / acc[64:65]
            r.linv[h, :, lanes] = inverse
            parts.append(acc[0:64] * inverse)
        ot = jnp.concatenate(parts, 0)
        r.ot[:, lanes] = ot
        r.o[rows(yy * 256, 256), :] = ot.T.astype(BF)
        x_o.start_pair(yy)

    r.orow[:, own_cols] = r.o[own, :]
    ag_cot.first()
    ag_cot.second()
    whole_wo.w4()
    x_o.wait()

    x = r.xb[...].astype(F32)
    y1 = x + nn(r.orow[...], r.wo[...])
    r.y1[...] = y1
    xhat, inverse = norm(y1)
    r.xhat2[...] = xhat
    r.inv2[...] = inverse
    r.h2[own, :] = (xhat * gain2[...]).astype(BF)
    ag_h2.start()
    x_o.sent()
    ag_cot.third()
    f_wg[0].wait()
    f_wg[1].wait()
    f_wm.wait()
    ag_cot.rest()

    def mix(yy):
        at = rows(yy * 256, 256)
        lanes = cols(yy * 256, 256)
        h2 = r.h2[at, :]
        a = nt(h2, r.wg[0])
        b = nt(h2, r.wg[1])
        cdf = 0.5 * (1.0 + lax.erf(a * 0.7071067811865476))
        gelu = a * cdf
        slope = cdf + a * (jnp.exp(-0.5 * a * a) * 0.3989422804014327)
        m = gelu * b
        dm = nt(r.cotb[at, :], r.wm[...]).astype(BF).astype(F32)
        da = dm * b * slope
        db = dm * gelu
        r.m[at, :] = m.astype(BF)
        r.da[at, :] = da.astype(BF)
        r.db[at, :] = db.astype(BF)
        r.mt[0:FF, lanes] = m.T.astype(BF)
        r.dat[0:FF, lanes] = da.T.astype(BF)
        r.dbt[0:FF, lanes] = db.T.astype(BF)

    ag_h2.steps(mix)

    def back_mix(yy):
        at = rows(yy * 256, 256)
        return nn(r.da[at, :], r.wg[0]) + nn(r.db[at, :], r.wg[1])

    rs_2 = scatter("r2")
    rs_2.phase(back_mix)
    sums_m = StagedPlaneSum(
        p, r.gm, r.gm_big, r.gm_res, r.gm_small, r.gm_mine, r.gm_out, r.s_sm, r.s_sm_back
    )

    def mix_grads(i):
        lanes = cols(i * 256, 256)
        grads = [
            nn(r.mt[...], r.cotb[:, lanes]).astype(BF),
            nn(r.dat[...], r.h2[:, lanes]).astype(BF),
            nn(r.dbt[...], r.h2[:, lanes]).astype(BF),
            jnp.zeros((1024 - 3 * FR, 256), BF),
        ]
        r.gm[:, :, :, lanes] = jnp.concatenate(grads, 0).reshape(4, 4, 64, 256)

    pl.loop(0, 2)(mix_grads)
    sums_m.first[0].start()
    rs_2.step1()
    pl.loop(2, 4)(mix_grads)
    sums_m.first[1].start()
    dh2 = rs_2.step2()

    dx, dgain2 = norm_back(dh2, r.xhat2[...], r.inv2[...], gain2[...])
    gy = r.cotb[own, :].astype(F32) + dx
    r.gy[...] = gy
    r.gb[own, :] = gy.astype(BF)
    r.dorow[...] = nt(r.gb[own, :], r.wo[...]).astype(BF)
    x_do = Exchange(p, lambda j: r.dorow.at[:, cols(j * B, B)], r.dob.at[own], r.dob, r.s_x_do)
    x_do.start()
    r.dob[own, :] = r.dorow[:, own_cols]
    ag_gb.start()
    gain_2 = Gain(p, r.g2t, r.g2p, r.s_g2)
    gain_2.start(dgain2)
    rs_o = scatter("ro")
    rs_o.phase(lambda yy: nn(r.m[rows(yy * 256, 256), :], r.wm[...]), False)

    @pl.loop(0, 4)
    def _(step):
        yy = (p.y + pick(step, 0, 3, 1, 2)) % 4
        at = rows(yy * 256, 256)
        lanes = cols(yy * 256, 256)
        x_do.wait_pair(yy)
        pl.when(step == 1)(lambda: sums_m.to_second(0))
        dot = r.dob[at, :].astype(F32).T
        zero = jnp.zeros((64, 256), BF)
        scaled = []
        for h in range(2):
            half = dot[h * 64 : h * 64 + 64] * r.linv[h, :, lanes]
            scaled.append(half)
        dpt = [
            nn(r.v[...], jnp.concatenate([scaled[0].astype(BF), zero], 0)),
            nn(r.v[...], jnp.concatenate([zero, scaled[1].astype(BF)], 0)),
        ]
        r.dos[at, :] = jnp.concatenate(scaled, 0).T.astype(BF)
        for h in range(2):
            half = slice(h * 64, h * 64 + 64)
            weighted = jnp.sum(scaled[h] * r.ot[half, lanes], 0, keepdims=True)
            ds = (r.pt[h, :, lanes].astype(F32) * (dpt[h] - weighted)).astype(BF)
            r.ds[h, :, lanes] = ds
            r.dqt[half, lanes] = nn(r.kt[half, :], ds)

    x_do.sent()
    sums_m.to_second(1)

    def back_project(yy):
        at = rows(yy * 256, 256)
        lanes = cols(yy * 256, 256)
        first = lax.broadcasted_iota(jnp.int32, (256, B), 1) < 64
        dk = jnp.where(first, nn(r.ds[0, at, :], r.q[...]), nn(r.ds[1, at, :], r.q[...])) * (1 / LOG2E)
        dv = jnp.where(first, nn(r.pt[0, at, :], r.dos[...]), nn(r.pt[1, at, :], r.dos[...]))
        co, si = cosine[at, :], signed[at, :]
        dq = r.dqt[:, lanes].T * 0.125
        dq = dq * co - swap_halves(dq) * si
        dk = dk * co - swap_halves(dk) * si
        r.dqkvt[0:128, lanes] = dq.T.astype(BF)
        r.dqkvt[128:256, lanes] = dk.T.astype(BF)
        r.dqkvt[256:384, lanes] = dv.T.astype(BF)
        r.dqkv[at, :] = jnp.concatenate([dq.astype(BF), dk.astype(BF), dv.astype(BF)], 1)

    pl.loop(0, 4)(back_project)

    def spread_out(full, i, off, grad):
        size = grad.shape[0] // 8
        full[:, pl.ds(2 * i, 2), :, off : off + 256] = grad.astype(BF).reshape(4, 2, size, 256)

    sums_a = PlaneSum(
        p, r.ga, r.ga_big, r.ga_res, r.ga_small, r.ga_mine, r.ga_out, r.s_sa, r.s_sa_back
    )
    for n in range(2):

        @pl.loop(0, 2)
        def _(i, off=256 * n):
            spread_out(r.ga, i, off, nn(r.dqkvt[...], r.h1[:, cols(i * 512 + off, 256)]))

        sums_a.first[n].start()

    gain_2.middle()
    sums_m.to_mine()
    sums_m.g0()
    ag_gb.first()
    ag_gb.second()
    rs_1 = scatter("r1")

    rs_1.phase(lambda yy: nn(r.dqkv[rows(yy * 256, 256), :], r.w[...]))
    rs_1.step1()
    sums_a.to_second(0, 1)
    sums_m.g1()
    ag_gb.third()
    ag_gb.rest()
    sums_o = PlaneSum(
        p, r.go, r.go_big, r.go_res, r.go_small, r.go_mine, r.go_out, r.s_so, r.s_so_back
    )
    for n in range(2):

        @pl.loop(0, 2)
        def _(i, off=256 * n):
            spread_out(r.go, i, off, nn(r.ot[...].astype(BF), r.gb[:, cols(i * 512 + off, 256)]))

        sums_o.first[n].start()

    rs_o.step0()
    rs_o.step_right()
    rs_o.step_left()
    dh1 = rs_1.step2()
    xhat, inverse = norm(r.xb[...].astype(F32))
    dx, dgain1 = norm_back(dh1, xhat, inverse, gain1[...])
    gain_1 = Gain(p, r.g1t, r.g1p, r.s_g1)
    gain_1.start(dgain1)
    r.tg_here[...] = (r.gy[...] + dx).astype(BF)
    sw_tg = Swap(p, r.tg_here, r.tg_out, r.s_sw_tg)
    sw_tg.start()
    sums_a.to_mine()
    sums_a.give()
    sums_o.to_second(0, 1)
    rs_o.step1()
    gain_1.middle()
    sums_m.g2()
    sums_o.to_mine()
    sums_o.give()
    sums_m.g3()
    r.lo_here[...] = (r.y1[...] + rs_o.step2()).astype(BF)
    sw_lo = Swap(p, r.lo_here, r.lo_out, r.s_sw_lo)
    sw_lo.start()
    sw_tg.wait()
    tg_copy = pltpu.make_async_copy(r.tg_out, tg_ref, r.s_outs.at[0])
    tg_copy.start()
    sums_m.finish()
    gm_copy = pltpu.make_async_copy(r.gm_out, gm_ref, r.s_outs.at[1])
    gm_copy.start()
    sums_a.take(ga_ref, r.s_outs.at[3])
    sums_o.take(go_ref, r.s_outs.at[4])
    sw_lo.wait()
    lo_copy = pltpu.make_async_copy(r.lo_out, lo_ref, r.s_outs.at[2])
    lo_copy.start()
    gains_ref[1:2, :] = gain_2.end()
    gains_ref[0:1, :] = gain_1.end()
    sums_a.taken()
    sums_o.taken()
    for copy in [lo_copy, tg_copy, gm_copy]:
        copy.wait()
    drain(r.ga_out, r.s_outs.at[3])
    drain(r.go_out, r.s_outs.at[4])


def widen(
    lo, tg, ga, go, gm, gains, lo_ref, tg_ref, gi_ref, go_ref, gg_ref, gm_ref, first_ref, second_ref,
    lo_in, tg_in, ga_in, go_in, gm_in, tg_out, ga_out, go_out, gm_out, sems,
):
    def whole(held, wide, first, size):
        wide[first : first + size, :] = held[first : first + size, :].astype(F32)

    def chunks(held, wide, first, size):
        size = size // 8
        for z in range(4):
            for x in range(4):
                group, half = (z * 2 + x % 2) * size, x // 2 * 512
                wide[group : group + size, half : half + 512] = held[z, x].astype(F32)

    pieces = [
        (go, go_in, go_out, 0, B, go_ref, chunks),
        (tg, tg_in, tg_out, 0, B, tg_ref, whole),
        (ga, ga_in, ga_out, 0, 384, gi_ref, chunks),
    ]
    targets = gm_ref, gg_ref.at[0], gg_ref.at[1]
    pieces += [(gm, gm_in, gm_out, i * FR, FF, target, whole) for i, target in enumerate(targets)]
    loads, stores = [], []
    for i, (src, held, _, first, size, _, _) in enumerate(pieces):
        if size == FF:
            src, held = src.at[pl.ds(first, FR)], held.at[pl.ds(first, FR)]
        loads.append(pltpu.make_async_copy(src, held, sems.at[i]))
    loads.append(pltpu.make_async_copy(lo, lo_in, sems.at[6]))
    for load in loads:
        load.start()
    for i in range(8):
        first_ref[i : i + 1, :] = gains[0:1, i * B : i * B + B]
        second_ref[i : i + 1, :] = gains[1:2, i * B : i * B + B]
    for i, (_, held, wide, first, size, target, convert) in enumerate(pieces):
        loads[i].wait()
        convert(held, wide, first, size)
        stores.append(pltpu.make_async_copy(wide.at[pl.ds(first, size)], target, sems.at[7 + i]))
        stores[-1].start()
    loads[6].wait()
    stores.append(pltpu.make_async_copy(lo_in, lo_ref, sems.at[13]))
    stores[-1].start()
    for store in stores:
        store.wait()


def local(tokens, attn_in, attn_out, mlp_in, mlp_out, norm_first, norm_second, cotangent):
    cosine, signed = tables()
    any_space = pl.BlockSpec(memory_space=pl.ANY)
    vmem = pl.BlockSpec(memory_space=pltpu.VMEM)
    limit = 63 * 1024 * 1024
    shapes = [(B, D), (B, D), (4, 4, 48, 512), (4, 4, 16, 512), (4, 4, 64, D)]
    lo, tg, ga, go, gm, gains = pl.pallas_call(
        kernel,
        out_shape=tuple(jax.ShapeDtypeStruct(shape, BF) for shape in shapes)
        + (jax.ShapeDtypeStruct((2, D), F32),),
        in_specs=[any_space] * 10,
        out_specs=(any_space,) * 5 + (vmem,),
        scratch_shapes=[pltpu.VMEM(shape, kind) for shape, kind in SCRATCH.values()]
        + [pltpu.SemaphoreType.DMA(shape) for shape in SEMS.values()],
        compiler_params=pltpu.CompilerParams(
            collective_id=0, has_side_effects=True, vmem_limit_bytes=limit
        ),
    )(
        tokens,
        cotangent,
        attn_in.transpose(1, 2, 3, 0).reshape(384, D),
        attn_out.reshape(B, D),
        mlp_in.transpose(0, 2, 1),
        mlp_out,
        norm_first.reshape(1, D),
        norm_second.reshape(1, D),
        jnp.asarray(cosine),
        jnp.asarray(signed),
    )
    wide = [(B, D), (384, D), (B, D), (2, FF, D), (FF, D), (8, B), (8, B)]
    lo, tg, gi, go, gg, gm, first, second = pl.pallas_call(
        widen,
        out_shape=(jax.ShapeDtypeStruct((B, D), BF),)
        + tuple(jax.ShapeDtypeStruct(shape, F32) for shape in wide),
        in_specs=[any_space] * 5 + [vmem],
        out_specs=(any_space,) * 6 + (vmem, vmem),
        scratch_shapes=[
            pltpu.VMEM((B, D), BF),
            pltpu.VMEM((B, D), BF),
            pltpu.VMEM((4, 4, 48, 512), BF),
            pltpu.VMEM((4, 4, 16, 512), BF),
            pltpu.VMEM((1024, D), BF),
            pltpu.VMEM((B, D), F32),
            pltpu.VMEM((384, D), F32),
            pltpu.VMEM((B, D), F32),
            pltpu.VMEM((3 * FR, D), F32),
            pltpu.SemaphoreType.DMA((14,)),
        ],
        compiler_params=pltpu.CompilerParams(vmem_limit_bytes=limit),
    )(lo, tg, ga, go, gm.reshape(1024, D), gains)
    return (
        lo,
        tg,
        gi.reshape(3, 2, 64, D).transpose(3, 0, 1, 2),
        go.reshape(2, 64, D),
        gg.transpose(0, 2, 1),
        gm,
        first.reshape(D),
        second.reshape(D),
    )


def solution(mesh):
    placed = (
        P(("dp", "tensor"), None),
        P(None, None, "tensor", None),
        P("tensor", None, None),
        P(None, None, "tensor"),
        P("tensor", None),
        P(),
        P(),
        P(("dp", "tensor"), None),
    )
    return jax.shard_map(
        local,
        mesh=mesh,
        in_specs=placed,
        out_specs=(
            P(("dp", "tensor"), None),
            P(("dp", "tensor"), None),
            P(None, None, "tensor", None),
            P("tensor", None, None),
            P(None, None, "tensor"),
            P("tensor", None),
            P(),
            P(),
        ),
        check_vma=False,
    )
```
